32 devices in a mesh: blk: 8 (over z, y), rep: 4 (over x, core).
Axes of the slice: x: 2, y: 2, z: 4, core: 2. Of those that a mesh axis runs over, the one named last changes fastest.
Arguments:
- features: bfloat16 [4096, 256], P('blk'), may hold values from -6 to 6
- weight: bfloat16 [256, 256], replicated, may hold values from -0.375 to 0.375
- cotangent: bfloat16 [4096, 256], P(('blk', 'rep')), may hold values from -6 to 6
- tile_values: bfloat16 [8, 8, 12, 128, 128], P('blk', 'rep'), may hold values from -0.15625 to 0.15625
- tile_rows: int32 [8, 8, 12], P('blk', 'rep'), may hold values from 0 to 3, as said below
- tile_cols: int32 [8, 8, 12], P('blk', 'rep'), may hold values from 0 to 3
- tile_count: int32 [8, 8], P('blk', 'rep'), may hold values from 1 to 12, as said below
Outputs:
- activations: bfloat16 [4096, 256], P(('blk', 'rep'))
- weight_grad: float32 [256, 256], replicated
- feature_grad: bfloat16 [4096, 256], P(('blk', 'rep'))
The draws below stay inside these ranges and needn't reach their ends.
Inputs may be any that keep to these rules, and one draw needn't show every extreme that they name: Among the live slots of one list the pairs (tile_rows, tile_cols) are distinct. `tile_count`: the list of a block with itself (offset 0) always has 12 live slots.
All inputs are finite; a program needn't handle non-finite values.
Results may differ from the reference program's by a relative error of at most 0.024.
Values may be sent and summed in bfloat16 or wider, within the bound.
A program may use at most 64 MiB of HBM per device.

```python
import math
import jax
import jax.numpy as jnp
from jax import lax

WIDTH = 256
ROWS = 512
SLOTS = 12
BLOCKS = 8
NODES = 4096


def tile_layout(key):
    row_tiles = ROWS // 128
    positions = row_tiles * row_tiles
    scores = jax.random.randint(key, (BLOCKS, BLOCKS, positions), 0, 1 << 20) * positions
    scores = scores + jnp.arange(positions, dtype=jnp.int32)
    order = jnp.argsort(scores, axis=-1)[..., :SLOTS].astype(jnp.int32)
    heavy = jax.random.randint(jax.random.fold_in(key, 1), (BLOCKS, 1), 0, SLOTS // 2 + 1)
    extra = jax.random.randint(jax.random.fold_in(key, 2), (BLOCKS, BLOCKS), 1, SLOTS // 2 + 1)
    count = jnp.clip(heavy + extra, 1, SLOTS).astype(jnp.int32)
    count = count.at[:, 0].set(SLOTS)
    return (order // row_tiles, order % row_tiles, count)


def draw_tile_rows(key, part):
    rows, cols, count = tile_layout(key)
    return rows.astype(jnp.int32)


def draw_tile_cols(key, part):
    rows, cols, count = tile_layout(key)
    return cols.astype(jnp.int32)


def draw_tile_count(key, part):
    rows, cols, count = tile_layout(key)
    return count.astype(jnp.int32)


def block_levels(stream_key, extent, pieces, least, high):
    def one(dim, shards_of):
        steps = jax.random.uniform(jax.random.fold_in(jax.random.fold_in(stream_key, 6), dim), (shards_of,), jnp.float32, least / len(pieces), high / len(pieces))
        return jnp.repeat(jnp.exp(steps), extent[dim] // shards_of).reshape((-1,) + (1,) * (len(extent) - dim - 1))

    gain = one(*pieces[0])
    for cut in pieces[1:]:
        gain = gain * one(*cut)
    return gain


def scatter_about(own_key, extent, width, limit, split=(), kind=jnp.bfloat16):
    entries = width * jax.random.normal(own_key, extent, jnp.float32)
    if split:
        entries = entries * block_levels(own_key, extent, split, -0.22, 0.18)
    return jnp.clip(entries, -limit, limit).astype(kind)


def setup_inputs(seed: int = 0) -> dict:
    key_list = jax.random.split(jax.random.key(seed), 8)
    return {
        "features": scatter_about(key_list[0], (NODES, WIDTH), 1.0, 6.0, ((0, 8),)),
        "weight": scatter_about(key_list[1], (WIDTH, WIDTH), WIDTH ** -0.5, 0.375),
        "cotangent": scatter_about(key_list[2], (NODES, WIDTH), 1.0, 6.0, ((0, 32),)),
        "tile_values": scatter_about(key_list[3], (BLOCKS, BLOCKS, SLOTS, 128, 128), (BLOCKS * SLOTS * 8192 // ROWS) ** -0.5, 0.15625, ((0, 8), (1, 4))),
        "tile_rows": draw_tile_rows(jax.random.fold_in(key_list[7], 71), 0),
        "tile_cols": draw_tile_cols(jax.random.fold_in(key_list[7], 71), 0),
        "tile_count": draw_tile_count(jax.random.fold_in(key_list[7], 71), 0),
    }


def aggregate(tile_values, tile_rows, tile_cols, tile_count, features):
    row_tiles = ROWS // 128
    blocks = features.reshape(BLOCKS, row_tiles, 128, WIDTH)
    slot_ids = jnp.arange(SLOTS, dtype=jnp.int32)
    offsets = jnp.arange(BLOCKS, dtype=jnp.int32)

    def one_block(index):
        rolled = jnp.roll(blocks, -index, axis=0)
        tiles = lax.dynamic_index_in_dim(tile_values, index, 0, False).astype(jnp.float32)
        rows = lax.dynamic_index_in_dim(tile_rows, index, 0, False)
        cols = lax.dynamic_index_in_dim(tile_cols, index, 0, False)
        count = lax.dynamic_index_in_dim(tile_count, index, 0, False)
        live = (slot_ids[None, :] < count[:, None]).astype(jnp.float32)
        picked = rolled[offsets[:, None], cols].astype(jnp.float32)
        product = jnp.einsum('osij,osjf->osif', tiles, picked, precision=lax.Precision.HIGHEST)
        product = product * live[:, :, None, None]
        row_hot = (rows[:, :, None] == jnp.arange(row_tiles, dtype=jnp.int32)).astype(jnp.float32)
        return jnp.einsum('osr,osif->rif', row_hot, product, precision=lax.Precision.HIGHEST)
    return lax.map(one_block, offsets).reshape(NODES, WIDTH)

def spread_back(tile_values, tile_rows, tile_cols, tile_count, grads):
    row_tiles = ROWS // 128
    blocks = grads.reshape(BLOCKS, row_tiles, 128, WIDTH)
    slot_ids = jnp.arange(SLOTS, dtype=jnp.int32)

    def step(total, index):
        tiles = lax.dynamic_index_in_dim(tile_values, index, 0, False).astype(jnp.float32)
        rows = lax.dynamic_index_in_dim(tile_rows, index, 0, False)
        cols = lax.dynamic_index_in_dim(tile_cols, index, 0, False)
        count = lax.dynamic_index_in_dim(tile_count, index, 0, False)
        live = (slot_ids[None, :] < count[:, None]).astype(jnp.float32)
        mine = lax.dynamic_index_in_dim(blocks, index, 0, False)
        picked = mine[rows].astype(jnp.float32)
        product = jnp.einsum('osij,osif->osjf', tiles, picked, precision=lax.Precision.HIGHEST)
        product = product * live[:, :, None, None]
        col_hot = (cols[:, :, None] == jnp.arange(row_tiles, dtype=jnp.int32)).astype(jnp.float32)
        contrib = jnp.einsum('osc,osjf->ocjf', col_hot, product, precision=lax.Precision.HIGHEST)
        return (total + jnp.roll(contrib, index, axis=0), None)
    start = jnp.zeros((BLOCKS, row_tiles, 128, WIDTH), jnp.float32)
    total, unused = lax.scan(step, start, jnp.arange(BLOCKS, dtype=jnp.int32))
    return total.reshape(NODES, WIDTH)

def reference(features, weight, cotangent, tile_values, tile_rows, tile_cols, tile_count):
    agg = aggregate(tile_values, tile_rows, tile_cols, tile_count, features).astype(jnp.bfloat16)
    z_value = jnp.dot(agg, weight, preferred_element_type=jnp.float32)
    sigma = jax.nn.sigmoid(z_value)
    activations = (z_value * sigma).astype(jnp.bfloat16)
    dz_value = (cotangent.astype(jnp.float32) * sigma * (1.0 + z_value * (1.0 - sigma))).astype(jnp.bfloat16)
    weight_grad = jnp.dot(agg.T, dz_value, preferred_element_type=jnp.float32) / math.sqrt(NODES)
    dy_value = jnp.dot(dz_value, weight.T, preferred_element_type=jnp.float32).astype(jnp.bfloat16)
    feature_grad = spread_back(tile_values, tile_rows, tile_cols, tile_count, dy_value).astype(jnp.bfloat16)
    return (activations, weight_grad, feature_grad)
```

```python
import functools
import math

import jax
import jax.numpy as jnp
from jax import lax
from jax.experimental import pallas as pl
from jax.experimental.pallas import tpu as pltpu
from jax.sharding import PartitionSpec as P

MESH = pl.DeviceIdType.MESH
TILE = 128
UNROLL = 8


def repeat(count, body, first=0):
    if count - first <= UNROLL:
        for index in range(first, count):
            body(index)
    else:

        def step(index, carry):
            body(index)
            return carry

        lax.fori_loop(first, count, step, 0)


def kernel(dims, *refs):
    blocks, replicas, sections, rows_blk, width, slots, own_rows, w_rows, w_chunk, nodes = dims
    (feat, weight, cot, tiles, trows, tcols, tcount) = refs[:7]
    (act, wgrad, fgrad) = refs[7:10]
    (fbuf, amat, amat_t, pbuf, rbuf, dzfull, agg_t, aggs, gbuf, gslots, wpart, wslots, wcol) = refs[10:23]
    (f_send, f_recv, p_send, p_recv, z_send, z_recv, a_send, a_recv) = refs[23:31]
    (g_send, g_recv, w_send, w_recv, c_send, c_recv, r_send, r_recv) = refs[31:]
    b = lax.axis_index("blk")
    r = lax.axis_index("rep")
    row_tiles = rows_blk // TILE
    whole_weight = w_chunk > 0

    def blk_at(offset):
        return lax.rem(b + offset + 2 * blocks, blocks)

    def remote(src, dst, send, recv, to):
        return pltpu.make_async_remote_copy(
            src_ref=src, dst_ref=dst, send_sem=send, recv_sem=recv, device_id=to, device_id_type=MESH
        )

    barrier = pltpu.get_barrier_semaphore()

    def greet(to):
        pl.semaphore_signal(barrier, inc=1, device_id=to, device_id_type=MESH)

    repeat(replicas, lambda d: greet((b, lax.rem(r + d, replicas))), 1)
    repeat(blocks, lambda d: greet((blk_at(d), r)), 1)

    def greet_grad(o):
        source = o // sections

        @pl.when(jnp.logical_or(o != 0, r != 0))
        def _():
            greet((blk_at(-o), source))

    repeat(blocks, greet_grad)
    own = jnp.where(r == 0, 1, 0)
    pl.semaphore_wait(barrier, replicas - 1 + blocks - 1 + sections * replicas - own)

    def feature_copy(s):
        return remote(
            feat, fbuf.at[s], f_send.at[s], f_recv.at[s], (blk_at(-(sections * r + s)), r)
        )

    for s in range(sections):
        if s == 0:

            @pl.when(r != 0)
            def _():
                feature_copy(0).start()

            @pl.when(r == 0)
            def _():
                fbuf[0] = feat[...]
        else:
            feature_copy(s).start()

    for s in range(sections):
        count = tcount[0, s]
        place = [
            jnp.where(t < count, trows[0, s, t] * row_tiles + tcols[0, s, t], -1)
            for t in range(slots)
        ]
        for i in range(row_tiles):
            for j in range(row_tiles):
                slot = jnp.int32(0)
                for t in range(slots):
                    slot = jnp.where(place[t] == i * row_tiles + j, t + 1, slot)
                tile = tiles[0, s, jnp.maximum(slot - 1, 0)]
                tile = jnp.where(slot > 0, tile, jnp.zeros_like(tile))
                at_row = pl.ds(i * TILE, TILE)
                at_col = pl.ds(s * rows_blk + j * TILE, TILE)
                amat[at_row, at_col] = tile
                amat_t[at_col, at_row] = tile.T

    for s in range(sections):
        if s == 0:

            @pl.when(r != 0)
            def _():
                feature_copy(0).wait()
        else:
            feature_copy(s).wait()

    def partial_rows(k):
        total = jnp.zeros((own_rows, width), jnp.float32)
        at_row = pl.ds(pl.multiple_of(k * own_rows, own_rows), own_rows)
        for s in range(sections):
            total = total + jnp.dot(
                amat[at_row, s * rows_blk : (s + 1) * rows_blk],
                fbuf[s],
                preferred_element_type=jnp.float32,
            )
        return total

    def partial_copy(d):
        return remote(
            pbuf.at[d - 1],
            rbuf.at[d - 1],
            p_send.at[d - 1],
            p_recv.at[d - 1],
            (b, lax.rem(r + d, replicas)),
        )

    def send_partial(d):
        pbuf[d - 1] = partial_rows(lax.rem(r + d, replicas)).astype(pbuf.dtype)
        partial_copy(d).start()

    repeat(replicas, send_partial, 1)
    total = partial_rows(r)
    repeat(replicas, lambda d: partial_copy(d).wait(), 1)
    for d in range(1, replicas):
        total = total + rbuf[d - 1].astype(jnp.float32)
    agg = total.astype(jnp.bfloat16)

    z_value = jnp.dot(agg, weight[...], preferred_element_type=jnp.float32)
    sigma = jax.nn.sigmoid(z_value)
    dz = (cot[...].astype(jnp.float32) * sigma * (1.0 + z_value * (1.0 - sigma))).astype(jnp.bfloat16)
    mine = pl.ds(pl.multiple_of(r * own_rows, own_rows), own_rows)
    dzfull[mine, :] = dz

    def dz_copy(d):
        return remote(
            dzfull.at[mine],
            dzfull.at[mine],
            z_send.at[d - 1],
            z_recv.at[d - 1],
            (b, lax.rem(r + d, replicas)),
        )

    def dz_arrival(d):
        source = lax.rem(r + replicas - d, replicas)
        at_row = pl.ds(pl.multiple_of(source * own_rows, own_rows), own_rows)
        return remote(
            dzfull.at[at_row], dzfull.at[at_row], z_send.at[d - 1], z_recv.at[d - 1], (b, source)
        )

    repeat(replicas, lambda d: dz_copy(d).start(), 1)
    agg_t[...] = agg.T

    def agg_copy(d):
        peer = lax.rem(r + d, replicas)
        at_row = pl.ds(pl.multiple_of(peer * w_rows, w_rows), w_rows)
        return remote(agg_t.at[at_row], aggs.at[d], a_send.at[d - 1], a_recv.at[d - 1], (b, peer))

    repeat(replicas, lambda d: agg_copy(d).start(), 1)
    aggs[0] = agg_t[pl.ds(pl.multiple_of(r * w_rows, w_rows), w_rows), :]
    act[...] = (z_value * sigma).astype(jnp.bfloat16)

    repeat(replicas, lambda d: dz_arrival(d).wait_recv(), 1)
    dy = lax.dot_general(
        dzfull[...], weight[...], (((1,), (1,)), ((), ())), preferred_element_type=jnp.float32
    ).astype(jnp.bfloat16)

    def grad_copy(s, k):
        o = sections * r + s
        return remote(
            gbuf.at[s, k], gslots.at[o], g_send.at[s, k], g_recv.at[o], (blk_at(o), k)
        )

    def send_grad(s, k):
        at_row = pl.ds(s * rows_blk + k * own_rows, own_rows)
        gbuf[s, k] = jnp.dot(amat_t[at_row, :], dy, preferred_element_type=jnp.float32).astype(
            gbuf.dtype
        )
        if s == 0 and k == 0:

            @pl.when(r != 0)
            def _():
                grad_copy(s, k).start()

            @pl.when(r == 0)
            def _():
                gslots[0] = gbuf[0, 0]
        else:
            grad_copy(s, k).start()

    def weight_rows():
        repeat(replicas, lambda d: agg_copy(d).wait_recv(), 1)
        acc = jnp.zeros((w_rows, width), jnp.float32)
        for d in range(replicas):
            source = lax.rem(r + replicas - d, replicas)
            at_row = pl.ds(pl.multiple_of(source * own_rows, own_rows), own_rows)
            acc = acc + jnp.dot(aggs[d], dzfull[at_row, :], preferred_element_type=jnp.float32)
        return acc * (1.0 / math.sqrt(nodes))

    def chunk_of(at):
        return pl.ds(pl.multiple_of(at * w_chunk, w_chunk), w_chunk)

    def w_copy(d):
        return remote(
            wpart.at[chunk_of(blk_at(d))], wslots.at[d - 1], w_send.at[d - 1], w_recv.at[d - 1], (blk_at(d), r)
        )

    def c_copy(d):
        return remote(
            wcol.at[chunk_of(b)], wcol.at[chunk_of(b)], c_send.at[d - 1], c_recv.at[d - 1], (blk_at(d), r)
        )

    def c_arrival(d):
        at_row = chunk_of(blk_at(-d))
        return remote(wcol.at[at_row], wcol.at[at_row], c_send.at[d - 1], c_recv.at[d - 1], (blk_at(-d), r))

    def r_copy(d):
        at_row = pl.ds(pl.multiple_of(r * w_rows, w_rows), w_rows)
        return remote(
            wcol, wgrad.at[at_row], r_send.at[d - 1], r_recv.at[d - 1], (b, lax.rem(r + d, replicas))
        )

    def r_arrival(d):
        source = lax.rem(r + replicas - d, replicas)
        at_row = pl.ds(pl.multiple_of(source * w_rows, w_rows), w_rows)
        return remote(wcol, wgrad.at[at_row], r_send.at[d - 1], r_recv.at[d - 1], (b, source))

    if whole_weight:
        wpart[...] = weight_rows()
        repeat(blocks, lambda d: w_copy(d).start(), 1)
    else:
        wgrad[...] = weight_rows()

    for s in reversed(range(sections)):
        for k in range(replicas):
            send_grad(s, k)

    if whole_weight:
        repeat(blocks, lambda d: w_copy(d).wait_recv(), 1)
        chunk = wpart[chunk_of(b), :]
        for d in range(1, blocks):
            chunk = chunk + wslots[d - 1]
        wcol[chunk_of(b), :] = chunk
        repeat(blocks, lambda d: c_copy(d).start(), 1)
        repeat(blocks, lambda d: c_arrival(d).wait_recv(), 1)
        repeat(replicas, lambda d: r_copy(d).start(), 1)
        wgrad[pl.ds(pl.multiple_of(r * w_rows, w_rows), w_rows), :] = wcol[...]

    def grad_arrival(o):
        copy = remote(
            gslots.at[o], gslots.at[o], g_send.at[0, 0], g_recv.at[o], (blk_at(-o), o // sections)
        )

        @pl.when(jnp.logical_or(o != 0, r != 0))
        def _():
            copy.wait_recv()

    repeat(blocks, grad_arrival)
    summed = gslots[0].astype(jnp.float32)
    for o in range(1, blocks):
        summed = summed + gslots[o].astype(jnp.float32)
    fgrad[...] = summed.astype(jnp.bfloat16)

    repeat(replicas, lambda d: dz_copy(d).wait_send(), 1)
    repeat(replicas, lambda d: agg_copy(d).wait_send(), 1)
    for s in range(sections):
        for k in range(replicas):
            if s == 0 and k == 0:

                @pl.when(r != 0)
                def _():
                    grad_copy(s, k).wait_send()
            else:
                grad_copy(s, k).wait_send()
    if whole_weight:
        repeat(blocks, lambda d: w_copy(d).wait_send(), 1)
        repeat(blocks, lambda d: c_copy(d).wait_send(), 1)
        repeat(replicas, lambda d: r_arrival(d).wait_recv(), 1)
        repeat(replicas, lambda d: r_copy(d).wait_send(), 1)


def per_device(features, weight, cotangent, tile_values, tile_rows, tile_cols, tile_count):
    rows_blk, width = features.shape
    sections, slots = tile_rows.shape[1:]
    replicas = lax.axis_size("rep")
    blocks = lax.axis_size("blk")
    nodes = rows_blk * blocks
    own_rows = rows_blk // replicas
    w_rows = width // replicas
    w_chunk = w_rows // blocks if w_rows % (8 * blocks) == 0 else 0
    dims = (blocks, replicas, sections, rows_blk, width, slots, own_rows, w_rows, w_chunk, nodes)
    bf16, f32 = jnp.bfloat16, jnp.float32
    vmem = pl.BlockSpec(memory_space=pltpu.VMEM)
    smem = pl.BlockSpec(memory_space=pltpu.SMEM)
    dma = pltpu.SemaphoreType.DMA
    others = max(replicas - 1, 1)
    act, wgrad, fgrad = pl.pallas_call(
        functools.partial(kernel, dims),
        out_shape=(
            jax.ShapeDtypeStruct((own_rows, width), bf16),
            jax.ShapeDtypeStruct((width if w_chunk else w_rows, width), f32),
            jax.ShapeDtypeStruct((own_rows, width), bf16),
        ),
        in_specs=[vmem] * 4 + [smem] * 3,
        out_specs=(vmem, vmem, vmem),
        scratch_shapes=[
            pltpu.VMEM((sections, rows_blk, width), bf16),
            pltpu.VMEM((rows_blk, sections * rows_blk), bf16),
            pltpu.VMEM((sections * rows_blk, rows_blk), bf16),
            pltpu.VMEM((others, own_rows, width), bf16),
            pltpu.VMEM((others, own_rows, width), bf16),
            pltpu.VMEM((rows_blk, width), bf16),
            pltpu.VMEM((width, own_rows), bf16),
            pltpu.VMEM((replicas, w_rows, own_rows), bf16),
            pltpu.VMEM((sections, replicas, own_rows, width), bf16),
            pltpu.VMEM((blocks, own_rows, width), bf16),
            pltpu.VMEM((w_rows, width), f32),
            pltpu.VMEM((blocks, max(w_chunk, 8), width), f32),
            pltpu.VMEM((w_rows, width), f32),
            dma((sections,)),
            dma((sections,)),
            dma((others,)),
            dma((others,)),
            dma((others,)),
            dma((others,)),
            dma((others,)),
            dma((others,)),
            dma((sections, replicas)),
            dma((blocks,)),
            dma((blocks,)),
            dma((blocks,)),
            dma((blocks,)),
            dma((blocks,)),
            dma((others,)),
            dma((others,)),
        ],
        compiler_params=pltpu.CompilerParams(
            collective_id=0, has_side_effects=True, vmem_limit_bytes=24 * 1024 * 1024
        ),
        name="graph_layer",
    )(features, weight, cotangent, tile_values, tile_rows, tile_cols, tile_count)
    if not w_chunk:
        wgrad = lax.all_gather(lax.psum(wgrad, "blk"), "rep", axis=0, tiled=True)
    return (act, wgrad, fgrad)


def solution(mesh):
    return jax.shard_map(
        per_device,
        mesh=mesh,
        in_specs=(
            P("blk", None),
            P(),
            P(("blk", "rep"), None),
            P("blk", "rep", None, None, None),
            P("blk", "rep", None),
            P("blk", "rep", None),
            P("blk", "rep"),
        ),
        out_specs=(P(("blk", "rep"), None), P(), P(("blk", "rep"), None)),
        check_vma=False,
    )
```

```python
import functools
import math

import jax
import jax.numpy as jnp
from jax import lax
from jax.experimental import pallas as pl
from jax.experimental.pallas import tpu as pltpu
from jax.sharding import PartitionSpec as P

MESH = pl.DeviceIdType.MESH
TILE = 128
UNROLL = 8


def repeat(count, body, first=0):
    if count - first <= UNROLL:
        for index in range(first, count):
            body(index)
    else:

        def step(index, carry):
            body(index)
            return carry

        lax.fori_loop(first, count, step, 0)


def kernel(dims, *refs):
    blocks, replicas, sections, rows_blk, width, slots, own_rows, w_rows, w_chunk, nodes = dims
    (feat, weight_hbm, cot_hbm, tiles_hbm, trows_hbm, tcols_hbm, tcount_hbm) = refs[:7]
    (act, wgrad, fgrad) = refs[7:10]
    (weight, cot, tiles, trows, tcols, tcount) = refs[10:16]
    (fbuf, amat, amat_t, pbuf, rbuf, dzfull, agg_t, aggs) = refs[16:24]
    (gsend, gpair, gbuf, gslots, wpart, wslots, wcol, l_sem) = refs[24:32]
    (f_send, f_recv, h_send, h_recv, p_send, p_recv, z_send, z_recv, a_send, a_recv) = refs[32:42]
    (o_send, o_recv, g_send, g_recv, w_send, w_recv, c_send, c_recv, r_send, r_recv) = refs[42:]
    b = lax.axis_index("blk")
    r = lax.axis_index("rep")
    odd = lax.rem(b, 2)
    pairs = sections // 2
    row_tiles = rows_blk // TILE
    column_parts = width // TILE
    whole_weight = w_chunk > 0

    def blk_at(offset):
        return lax.rem(b + offset + 2 * blocks, blocks)

    def remote(src, dst, send, recv, to):
        return pltpu.make_async_remote_copy(
            src_ref=src, dst_ref=dst, send_sem=send, recv_sem=recv, device_id=to, device_id_type=MESH
        )

    local = [
        pltpu.make_async_copy(src, dst, l_sem.at[n])
        for n, (src, dst) in enumerate(
            (
                (trows_hbm, trows),
                (tcols_hbm, tcols),
                (tcount_hbm, tcount),
                (tiles_hbm, tiles),
                (weight_hbm, weight),
                (cot_hbm, cot),
            )
        )
    ]
    for copy in local:
        copy.start()

    barrier = pltpu.get_barrier_semaphore()

    def greet(to):
        pl.semaphore_signal(barrier, inc=1, device_id=to, device_id_type=MESH)

    neighbour = b + 1 - 2 * odd
    repeat(replicas, lambda d: greet((b, lax.rem(r + d, replicas))), 1)
    repeat(blocks, lambda d: greet((blk_at(d), r)), 1)
    greet((neighbour, lax.rem(r + 2 * odd - 1 + replicas, replicas)))

    def greet_grad(j):
        @pl.when(jnp.logical_or(j != 0, r != 0))
        def _():
            greet((blk_at(-2 * j), 2 * j // sections))

    repeat(blocks // 2, greet_grad)
    own = jnp.where(r == 0, 1, 0)
    pl.semaphore_wait(barrier, replicas + blocks - 1 + pairs * replicas - own)

    def columns(c):
        return pl.ds(c * TILE, TILE)

    def feature_copy(t, c):
        return remote(
            feat.at[:, columns(c)],
            fbuf.at[2 * t, c],
            f_send.at[t, c],
            f_recv.at[t, c],
            (blk_at(-(sections * r + 2 * t)), r),
        )

    def feature_local(c):
        return pltpu.make_async_copy(feat.at[:, columns(c)], fbuf.at[0, c], f_recv.at[0, c])

    def hand_copy(t, c):
        section = lax.rem(2 * t + 2 * odd - 1 + sections, sections)
        back = jnp.where(odd == 0, 1, 0) if t == 0 else 0
        return remote(
            fbuf.at[2 * t, c],
            fbuf.at[section, c],
            h_send.at[t, c],
            h_recv.at[section // 2, c],
            (neighbour, lax.rem(r - back + replicas, replicas)),
        )

    def hand_arrival(t, c):
        here = fbuf.at[2 * t + 1, c]
        return remote(here, here, h_send.at[t, c], h_recv.at[t, c], (neighbour, r))

    for c in range(column_parts):
        for t in range(pairs):
            if t == 0:

                @pl.when(r != 0)
                def _():
                    feature_copy(0, c).start()

                @pl.when(r == 0)
                def _():
                    feature_local(c).start()
            else:
                feature_copy(t, c).start()

    for copy in local[:4]:
        copy.wait()
    for s in range(sections):
        count = tcount[0, s]
        place = [
            jnp.where(t < count, trows[0, s, t] * row_tiles + tcols[0, s, t], -1)
            for t in range(slots)
        ]
        for i in range(row_tiles):
            for j in range(row_tiles):
                slot = jnp.int32(0)
                for t in range(slots):
                    slot = jnp.where(place[t] == i * row_tiles + j, t + 1, slot)
                tile = tiles[0, s, jnp.maximum(slot - 1, 0)]
                tile = jnp.where(slot > 0, tile, jnp.zeros_like(tile))
                at_row = pl.ds(i * TILE, TILE)
                at_col = pl.ds(s * rows_blk + j * TILE, TILE)
                amat[at_row, at_col] = tile
                amat_t[at_col, at_row] = tile.T

    for c in range(column_parts):
        for t in range(pairs):
            if t == 0:

                @pl.when(r != 0)
                def _():
                    feature_copy(0, c).wait()

                @pl.when(r == 0)
                def _():
                    feature_local(c).wait()
            else:
                feature_copy(t, c).wait()
            hand_copy(t, c).start()

    def partial_rows(k, c):
        total = jnp.zeros((own_rows, TILE), jnp.float32)
        at_row = pl.ds(pl.multiple_of(k * own_rows, own_rows), own_rows)
        for s in range(sections):
            total = total + jnp.dot(
                amat[at_row, s * rows_blk : (s + 1) * rows_blk],
                fbuf[s, c],
                preferred_element_type=jnp.float32,
            )
        return total

    def partial_copy(d, c):
        return remote(
            pbuf.at[d - 1, c],
            rbuf.at[d - 1, c],
            p_send.at[d - 1, c],
            p_recv.at[d - 1, c],
            (b, lax.rem(r + d, replicas)),
        )

    def send_partial(d, c):
        pbuf[d - 1, c] = partial_rows(lax.rem(r + d, replicas), c).astype(pbuf.dtype)
        partial_copy(d, c).start()

    totals = []
    for c in range(column_parts):
        for t in range(pairs):
            hand_arrival(t, c).wait_recv()
        repeat(replicas, lambda d: send_partial(d, c), 1)
        totals.append(partial_rows(r, c))
    for copy in local[4:]:
        copy.wait()
    for c in range(column_parts):
        repeat(replicas, lambda d: partial_copy(d, c).wait(), 1)
        for d in range(1, replicas):
            totals[c] = totals[c] + rbuf[d - 1, c].astype(jnp.float32)
    agg = jnp.concatenate(totals, axis=1).astype(jnp.bfloat16)

    z_value = jnp.dot(agg, weight[...], preferred_element_type=jnp.float32)
    sigma = jax.nn.sigmoid(z_value)
    dz = (cot[...].astype(jnp.float32) * sigma * (1.0 + z_value * (1.0 - sigma))).astype(jnp.bfloat16)
    mine = pl.ds(pl.multiple_of(r * own_rows, own_rows), own_rows)
    dzfull[mine, :] = dz

    def dz_copy(d):
        return remote(
            dzfull.at[mine],
            dzfull.at[mine],
            z_send.at[d - 1],
            z_recv.at[d - 1],
            (b, lax.rem(r + d, replicas)),
        )

    def dz_arrival(d):
        source = lax.rem(r + replicas - d, replicas)
        at_row = pl.ds(pl.multiple_of(source * own_rows, own_rows), own_rows)
        return remote(
            dzfull.at[at_row], dzfull.at[at_row], z_send.at[d - 1], z_recv.at[d - 1], (b, source)
        )

    repeat(replicas, lambda d: dz_copy(d).start(), 1)
    agg_t[...] = agg.T

    def agg_copy(d):
        peer = lax.rem(r + d, replicas)
        at_row = pl.ds(pl.multiple_of(peer * w_rows, w_rows), w_rows)
        return remote(agg_t.at[at_row], aggs.at[d], a_send.at[d - 1], a_recv.at[d - 1], (b, peer))

    repeat(replicas, lambda d: agg_copy(d).start(), 1)
    aggs[0] = agg_t[pl.ds(pl.multiple_of(r * w_rows, w_rows), w_rows), :]
    act[...] = (z_value * sigma).astype(jnp.bfloat16)

    repeat(replicas, lambda d: dz_arrival(d).wait_recv(), 1)
    dy = lax.dot_general(
        dzfull[...], weight[...], (((1,), (1,)), ((), ())), preferred_element_type=jnp.float32
    ).astype(jnp.bfloat16)

    def grad_rows(s, k):
        at_row = pl.ds(s * rows_blk + k * own_rows, own_rows)
        return jnp.dot(amat_t[at_row, :], dy, preferred_element_type=jnp.float32)

    def odd_copy(t, k):
        slot = lax.rem(t + odd, pairs)
        ahead = odd if t == pairs - 1 else 0
        return remote(
            gsend.at[t, k],
            gpair.at[slot, k],
            o_send.at[t, k],
            o_recv.at[slot, k],
            (neighbour, lax.rem(r + ahead, replicas)),
        )

    def odd_arrival(t, k):
        here = gpair.at[t, k]
        return remote(here, here, o_send.at[t, k], o_recv.at[t, k], (neighbour, r))

    def grad_copy(t, k):
        j = pairs * r + t
        return remote(
            gbuf.at[t, k], gslots.at[j], g_send.at[t, k], g_recv.at[j], (blk_at(2 * j), k)
        )

    def send_grad(t, k):
        term = grad_rows(2 * t, k)
        odd_arrival(t, k).wait_recv()
        gbuf[t, k] = (term + gpair[t, k].astype(jnp.float32)).astype(gbuf.dtype)
        if t == 0 and k == 0:

            @pl.when(r != 0)
            def _():
                grad_copy(t, k).start()

            @pl.when(r == 0)
            def _():
                gslots[0] = gbuf[0, 0]
        else:
            grad_copy(t, k).start()

    def weight_rows():
        repeat(replicas, lambda d: agg_copy(d).wait_recv(), 1)
        acc = jnp.zeros((w_rows, width), jnp.float32)
        for d in range(replicas):
            source = lax.rem(r + replicas - d, replicas)
            at_row = pl.ds(pl.multiple_of(source * own_rows, own_rows), own_rows)
            acc = acc + jnp.dot(aggs[d], dzfull[at_row, :], preferred_element_type=jnp.float32)
        return acc * (1.0 / math.sqrt(nodes))

    def chunk_of(at):
        return pl.ds(pl.multiple_of(at * w_chunk, w_chunk), w_chunk)

    def w_copy(d):
        return remote(
            wpart.at[chunk_of(blk_at(d))], wslots.at[d - 1], w_send.at[d - 1], w_recv.at[d - 1], (blk_at(d), r)
        )

    def c_copy(d):
        return remote(
            wcol.at[chunk_of(b)], wcol.at[chunk_of(b)], c_send.at[d - 1], c_recv.at[d - 1], (blk_at(d), r)
        )

    def c_arrival(d):
        at_row = chunk_of(blk_at(-d))
        return remote(wcol.at[at_row], wcol.at[at_row], c_send.at[d - 1], c_recv.at[d - 1], (blk_at(-d), r))

    def r_copy(d):
        at_row = pl.ds(pl.multiple_of(r * w_rows, w_rows), w_rows)
        return remote(
            wcol, wgrad.at[at_row], r_send.at[d - 1], r_recv.at[d - 1], (b, lax.rem(r + d, replicas))
        )

    def r_arrival(d):
        source = lax.rem(r + replicas - d, replicas)
        at_row = pl.ds(pl.multiple_of(source * w_rows, w_rows), w_rows)
        return remote(wcol, wgrad.at[at_row], r_send.at[d - 1], r_recv.at[d - 1], (b, source))

    for t in range(pairs):
        for k in range(replicas):
            gsend[t, k] = grad_rows(2 * t + 1, k).astype(gsend.dtype)
            odd_copy(t, k).start()

    if whole_weight:
        wpart[...] = weight_rows()
        repeat(blocks, lambda d: w_copy(d).start(), 1)
    else:
        wgrad[...] = weight_rows()

    for t in range(pairs):
        for k in range(replicas):
            send_grad(t, k)

    if whole_weight:
        repeat(blocks, lambda d: w_copy(d).wait_recv(), 1)
        chunk = wpart[chunk_of(b), :]
        for d in range(1, blocks):
            chunk = chunk + wslots[d - 1]
        wcol[chunk_of(b), :] = chunk
        repeat(blocks, lambda d: c_copy(d).start(), 1)
        repeat(blocks, lambda d: c_arrival(d).wait_recv(), 1)
        repeat(replicas, lambda d: r_copy(d).start(), 1)
        wgrad[pl.ds(pl.multiple_of(r * w_rows, w_rows), w_rows), :] = wcol[...]

    def grad_arrival(j):
        copy = remote(
            gslots.at[j], gslots.at[j], g_send.at[0, 0], g_recv.at[j], (blk_at(-2 * j), j // pairs)
        )

        @pl.when(jnp.logical_or(j != 0, r != 0))
        def _():
            copy.wait_recv()

    repeat(blocks // 2, grad_arrival)
    summed = gslots[0].astype(jnp.float32)
    for j in range(1, blocks // 2):
        summed = summed + gslots[j].astype(jnp.float32)
    fgrad[...] = summed.astype(jnp.bfloat16)

    for t in range(pairs):
        for c in range(column_parts):
            hand_copy(t, c).wait_send()
    repeat(replicas, lambda d: dz_copy(d).wait_send(), 1)
    repeat(replicas, lambda d: agg_copy(d).wait_send(), 1)
    for t in range(pairs):
        for k in range(replicas):
            odd_copy(t, k).wait_send()
            if t == 0 and k == 0:

                @pl.when(r != 0)
                def _():
                    grad_copy(t, k).wait_send()
            else:
                grad_copy(t, k).wait_send()
    if whole_weight:
        repeat(blocks, lambda d: w_copy(d).wait_send(), 1)
        repeat(blocks, lambda d: c_copy(d).wait_send(), 1)
        repeat(replicas, lambda d: r_arrival(d).wait_recv(), 1)
        repeat(replicas, lambda d: r_copy(d).wait_send(), 1)


def per_device(features, weight, cotangent, tile_values, tile_rows, tile_cols, tile_count):
    rows_blk, width = features.shape
    sections, slots = tile_rows.shape[1:]
    replicas = lax.axis_size("rep")
    blocks = lax.axis_size("blk")
    nodes = rows_blk * blocks
    own_rows = rows_blk // replicas
    w_rows = width // replicas
    w_chunk = w_rows // blocks if w_rows % (8 * blocks) == 0 else 0
    dims = (blocks, replicas, sections, rows_blk, width, slots, own_rows, w_rows, w_chunk, nodes)
    bf16, f32 = jnp.bfloat16, jnp.float32
    vmem = pl.BlockSpec(memory_space=pltpu.VMEM)
    dma = pltpu.SemaphoreType.DMA
    others = max(replicas - 1, 1)
    pairs, parts = sections // 2, width // TILE
    act, wgrad, fgrad = pl.pallas_call(
        functools.partial(kernel, dims),
        out_shape=(
            jax.ShapeDtypeStruct((own_rows, width), bf16),
            jax.ShapeDtypeStruct((width if w_chunk else w_rows, width), f32),
            jax.ShapeDtypeStruct((own_rows, width), bf16),
        ),
        in_specs=[pl.BlockSpec(memory_space=pl.ANY)] * 7,
        out_specs=(vmem, vmem, vmem),
        scratch_shapes=[
            pltpu.VMEM(weight.shape, bf16),
            pltpu.VMEM(cotangent.shape, bf16),
            pltpu.VMEM(tile_values.shape, bf16),
            pltpu.SMEM(tile_rows.shape, jnp.int32),
            pltpu.SMEM(tile_cols.shape, jnp.int32),
            pltpu.SMEM(tile_count.shape, jnp.int32),
            pltpu.VMEM((sections, parts, rows_blk, TILE), bf16),
            pltpu.VMEM((rows_blk, sections * rows_blk), bf16),
            pltpu.VMEM((sections * rows_blk, rows_blk), bf16),
            pltpu.VMEM((others, parts, own_rows, TILE), bf16),
            pltpu.VMEM((others, parts, own_rows, TILE), bf16),
            pltpu.VMEM((rows_blk, width), bf16),
            pltpu.VMEM((width, own_rows), bf16),
            pltpu.VMEM((replicas, w_rows, own_rows), bf16),
            pltpu.VMEM((pairs, replicas, own_rows, width), bf16),
            pltpu.VMEM((pairs, replicas, own_rows, width), bf16),
            pltpu.VMEM((pairs, replicas, own_rows, width), bf16),
            pltpu.VMEM((blocks // 2, own_rows, width), bf16),
            pltpu.VMEM((w_rows, width), f32),
            pltpu.VMEM((blocks, max(w_chunk, 8), width), f32),
            pltpu.VMEM((w_rows, width), f32),
            dma((6,)),
            dma((pairs, parts)),
            dma((pairs, parts)),
            dma((pairs, parts)),
            dma((pairs, parts)),
            dma((others, parts)),
            dma((others, parts)),
            dma((others,)),
            dma((others,)),
            dma((others,)),
            dma((others,)),
            dma((pairs, replicas)),
            dma((pairs, replicas)),
            dma((pairs, replicas)),
            dma((blocks // 2,)),
            dma((blocks,)),
            dma((blocks,)),
            dma((blocks,)),
            dma((blocks,)),
            dma((others,)),
            dma((others,)),
        ],
        compiler_params=pltpu.CompilerParams(
            collective_id=0, has_side_effects=True, vmem_limit_bytes=48 * 1024 * 1024
        ),
        name="graph_layer",
    )(features, weight, cotangent, tile_values, tile_rows, tile_cols, tile_count)
    if not w_chunk:
        wgrad = lax.all_gather(lax.psum(wgrad, "blk"), "rep", axis=0, tiled=True)
    return (act, wgrad, fgrad)


def solution(mesh):
    return jax.shard_map(
        per_device,
        mesh=mesh,
        in_specs=(
            P("blk", None),
            P(),
            P(("blk", "rep"), None),
            P("blk", "rep", None, None, None),
            P("blk", "rep", None),
            P("blk", "rep", None),
            P("blk", "rep"),
        ),
        out_specs=(P(("blk", "rep"), None), P(), P(("blk", "rep"), None)),
        check_vma=False,
    )
```

```python
import functools
import math

import jax
import jax.numpy as jnp
from jax import lax
from jax.experimental import pallas as pl
from jax.experimental.pallas import tpu as pltpu
from jax.sharding import PartitionSpec as P

MESH = pl.DeviceIdType.MESH
TILE = 128
UNROLL = 8
HALVES = 2


def repeat(count, body, first=0):
    if count - first <= UNROLL:
        for index in range(first, count):
            body(index)
    else:

        def step(index, carry):
            body(index)
            return carry

        lax.fori_loop(first, count, step, 0)


def kernel(dims, *refs):
    blocks, replicas, sections, rows_blk, width, slots, own_rows, w_rows, w_chunk, nodes = dims
    (feat, weight_hbm, cot_hbm, tiles_hbm, trows_hbm, tcols_hbm, tcount_hbm) = refs[:7]
    (act, wgrad, fgrad) = refs[7:10]
    (weight, cot, tiles, trows, tcols, tcount) = refs[10:16]
    (fbuf, amat, amat_t, pbuf, rbuf, dzfull, agg_t, aggs) = refs[16:24]
    (gsend, gpair, gbuf, gslots, wpart, wslots, wcol) = refs[24:31]
    (pfull, weight_t, gterm, l_sem) = refs[31:35]
    (f_send, f_recv, h_send, h_recv, p_send, p_recv, z_send, z_recv, a_send, a_recv) = refs[35:45]
    (o_send, o_recv, g_send, g_recv, w_send, w_recv, c_send, c_recv, r_send, r_recv) = refs[45:]
    b = lax.axis_index("blk")
    r = lax.axis_index("rep")
    odd = lax.rem(b, 2)
    pairs = sections // 2
    row_tiles = rows_blk // TILE
    column_parts = width // TILE
    whole_weight = w_chunk > 0
    pieces = [(c, h) for c in range(column_parts) for h in range(HALVES)]

    def blk_at(offset):
        return lax.rem(b + offset + 2 * blocks, blocks)

    def remote(src, dst, send, recv, to):
        return pltpu.make_async_remote_copy(
            src_ref=src, dst_ref=dst, send_sem=send, recv_sem=recv, device_id=to, device_id_type=MESH
        )

    local = [
        pltpu.make_async_copy(src, dst, l_sem.at[n])
        for n, (src, dst) in enumerate(
            (
                (trows_hbm, trows),
                (tcols_hbm, tcols),
                (tcount_hbm, tcount),
                (tiles_hbm, tiles),
                (weight_hbm, weight),
                (cot_hbm, cot),
            )
        )
    ]
    for copy in local:
        copy.start()

    barrier = pltpu.get_barrier_semaphore()

    def greet(to):
        pl.semaphore_signal(barrier, inc=1, device_id=to, device_id_type=MESH)

    neighbour = b + 1 - 2 * odd
    repeat(replicas, lambda d: greet((b, lax.rem(r + d, replicas))), 1)
    repeat(blocks, lambda d: greet((blk_at(d), r)), 1)
    greet((neighbour, lax.rem(r + 2 * odd - 1 + replicas, replicas)))

    def greet_grad(j):
        @pl.when(jnp.logical_or(j != 0, r != 0))
        def _():
            greet((blk_at(-2 * j), 2 * j // sections))

    repeat(blocks // 2, greet_grad)
    own = jnp.where(r == 0, 1, 0)
    pl.semaphore_wait(barrier, replicas + blocks - 1 + pairs * replicas - own)

    half_rows = rows_blk // HALVES

    def piece(section, c, h):
        return fbuf.at[section, c, pl.ds(h * half_rows, half_rows)]

    def feature_piece(c, h):
        return feat.at[pl.ds(h * half_rows, half_rows), pl.ds(c * TILE, TILE)]

    def feature_copy(t, c, h):
        return remote(
            feature_piece(c, h),
            piece(2 * t, c, h),
            f_send.at[t, c, h],
            f_recv.at[t, c, h],
            (blk_at(-(sections * r + 2 * t)), r),
        )

    def feature_local(c, h):
        return pltpu.make_async_copy(feature_piece(c, h), piece(0, c, h), f_recv.at[0, c, h])

    def hand_copy(t, c, h):
        section = lax.rem(2 * t + 2 * odd - 1 + sections, sections)
        back = jnp.where(odd == 0, 1, 0) if t == 0 else 0
        return remote(
            piece(2 * t, c, h),
            piece(section, c, h),
            h_send.at[t, c, h],
            h_recv.at[section // 2, c, h],
            (neighbour, lax.rem(r - back + replicas, replicas)),
        )

    def hand_arrival(t, c, h):
        here = piece(2 * t + 1, c, h)
        return remote(here, here, h_send.at[t, c, h], h_recv.at[t, c, h], (neighbour, r))

    for c, h in pieces:
        for t in range(pairs):
            if t == 0:

                @pl.when(r != 0)
                def _():
                    feature_copy(0, c, h).start()

                @pl.when(r == 0)
                def _():
                    feature_local(c, h).start()
            else:
                feature_copy(t, c, h).start()

    for copy in local[:4]:
        copy.wait()

    def place_tiles(s):
        count = tcount[0, s]
        place = [
            jnp.where(t < count, trows[0, s, t] * row_tiles + tcols[0, s, t], -1)
            for t in range(slots)
        ]
        for i in range(row_tiles):
            for j in range(row_tiles):
                slot = jnp.int32(0)
                for t in range(slots):
                    slot = jnp.where(place[t] == i * row_tiles + j, t + 1, slot)
                tile = tiles[0, s, jnp.maximum(slot - 1, 0)]
                tile = jnp.where(slot > 0, tile, jnp.zeros_like(tile))
                at_col = pl.ds(s * rows_blk + j * TILE, TILE)
                amat[pl.ds(i * TILE, TILE), at_col] = tile

    def turn_tiles(s):
        for i in range(row_tiles):
            for j in range(row_tiles):
                at_row = pl.ds(i * TILE, TILE)
                at_col = pl.ds(s * rows_blk + j * TILE, TILE)
                amat_t[at_col, at_row] = amat[at_row, at_col].T

    for s in range(pairs):
        place_tiles(s)
    for n, (c, h) in enumerate(pieces):
        for t in range(pairs):
            if t == 0:

                @pl.when(r != 0)
                def _():
                    feature_copy(0, c, h).wait()

                @pl.when(r == 0)
                def _():
                    feature_local(c, h).wait()
            else:
                feature_copy(t, c, h).wait()
            hand_copy(t, c, h).start()
        if n == 0:
            for s in range(pairs, sections):
                place_tiles(s)

    def rows_of(k):
        return pl.ds(pl.multiple_of(k * own_rows, own_rows), own_rows)

    def partial_copy(d, c):
        peer = lax.rem(r + d, replicas)
        return remote(
            pbuf.at[c, rows_of(peer)],
            rbuf.at[d - 1, c],
            p_send.at[d - 1, c],
            p_recv.at[d - 1, c],
            (b, peer),
        )

    totals = []
    for c in range(column_parts):
        for h in range(HALVES):
            for t in range(pairs):
                hand_arrival(t, c, h).wait_recv()
        product = jnp.zeros((rows_blk, TILE), jnp.float32)
        for s in range(sections):
            product = product + jnp.dot(
                amat[:, s * rows_blk : (s + 1) * rows_blk],
                fbuf[s, c],
                preferred_element_type=jnp.float32,
            )
        pbuf[c] = product.astype(pbuf.dtype)
        repeat(replicas, lambda d: partial_copy(d, c).start(), 1)
        pfull[...] = product
        totals.append(pfull[rows_of(r), :])
    for s in range(1, sections, 2):
        turn_tiles(s)
    for copy in local[4:]:
        copy.wait()
    weight_t[...] = weight[...].T
    for c in range(column_parts):
        repeat(replicas, lambda d: partial_copy(d, c).wait(), 1)
        for d in range(1, replicas):
            totals[c] = totals[c] + rbuf[d - 1, c].astype(jnp.float32)
    agg = jnp.concatenate(totals, axis=1).astype(jnp.bfloat16)

    z_value = jnp.dot(agg, weight[...], preferred_element_type=jnp.float32)
    sigma = jax.nn.sigmoid(z_value)
    dz = (cot[...].astype(jnp.float32) * sigma * (1.0 + z_value * (1.0 - sigma))).astype(jnp.bfloat16)
    mine = pl.ds(pl.multiple_of(r * own_rows, own_rows), own_rows)
    dzfull[mine, :] = dz

    def dz_copy(d):
        return remote(
            dzfull.at[mine],
            dzfull.at[mine],
            z_send.at[d - 1],
            z_recv.at[d - 1],
            (b, lax.rem(r + d, replicas)),
        )

    def dz_arrival(d):
        source = lax.rem(r + replicas - d, replicas)
        at_row = pl.ds(pl.multiple_of(source * own_rows, own_rows), own_rows)
        return remote(
            dzfull.at[at_row], dzfull.at[at_row], z_send.at[d - 1], z_recv.at[d - 1], (b, source)
        )

    repeat(replicas, lambda d: dz_copy(d).start(), 1)
    agg_t[...] = agg.T

    def agg_copy(d):
        peer = lax.rem(r + d, replicas)
        at_row = pl.ds(pl.multiple_of(peer * w_rows, w_rows), w_rows)
        return remote(agg_t.at[at_row], aggs.at[d], a_send.at[d - 1], a_recv.at[d - 1], (b, peer))

    repeat(replicas, lambda d: agg_copy(d).start(), 1)
    aggs[0] = agg_t[pl.ds(pl.multiple_of(r * w_rows, w_rows), w_rows), :]
    act[...] = (z_value * sigma).astype(jnp.bfloat16)
    for s in range(0, sections, 2):
        turn_tiles(s)

    repeat(replicas, lambda d: dz_arrival(d).wait_recv(), 1)
    dy = jnp.dot(dzfull[...], weight_t[...], preferred_element_type=jnp.float32).astype(jnp.bfloat16)

    def grad_terms(s):
        at_row = pl.ds(s * rows_blk, rows_blk)
        return jnp.dot(amat_t[at_row, :], dy, preferred_element_type=jnp.float32)

    def odd_copy(t, k):
        slot = lax.rem(t + odd, pairs)
        ahead = odd if t == pairs - 1 else 0
        return remote(
            gsend.at[t, k],
            gpair.at[slot, k],
            o_send.at[t, k],
            o_recv.at[slot, k],
            (neighbour, lax.rem(r + ahead, replicas)),
        )

    def odd_arrival(t, k):
        here = gpair.at[t, k]
        return remote(here, here, o_send.at[t, k], o_recv.at[t, k], (neighbour, r))

    def grad_copy(t, k):
        j = pairs * r + t
        return remote(
            gbuf.at[t, k], gslots.at[j], g_send.at[t, k], g_recv.at[j], (blk_at(2 * j), k)
        )

    def send_grad(t, k):
        term = gterm[t, k]
        odd_arrival(t, k).wait_recv()
        gbuf[t, k] = (term + gpair[t, k].astype(jnp.float32)).astype(gbuf.dtype)
        if t == 0 and k == 0:

            @pl.when(r != 0)
            def _():
                grad_copy(t, k).start()

            @pl.when(r == 0)
            def _():
                gslots[0] = gbuf[0, 0]
        else:
            grad_copy(t, k).start()

    def weight_rows():
        repeat(replicas, lambda d: agg_copy(d).wait_recv(), 1)
        acc = jnp.zeros((w_rows, width), jnp.float32)
        for d in range(replicas):
            source = lax.rem(r + replicas - d, replicas)
            at_row = pl.ds(pl.multiple_of(source * own_rows, own_rows), own_rows)
            acc = acc + jnp.dot(aggs[d], dzfull[at_row, :], preferred_element_type=jnp.float32)
        return acc * (1.0 / math.sqrt(nodes))

    def chunk_of(at):
        return pl.ds(pl.multiple_of(at * w_chunk, w_chunk), w_chunk)

    def w_copy(d):
        return remote(
            wpart.at[chunk_of(blk_at(d))], wslots.at[d - 1], w_send.at[d - 1], w_recv.at[d - 1], (blk_at(d), r)
        )

    def c_copy(d):
        return remote(
            wcol.at[chunk_of(b)], wcol.at[chunk_of(b)], c_send.at[d - 1], c_recv.at[d - 1], (blk_at(d), r)
        )

    def c_arrival(d):
        at_row = chunk_of(blk_at(-d))
        return remote(wcol.at[at_row], wcol.at[at_row], c_send.at[d - 1], c_recv.at[d - 1], (blk_at(-d), r))

    def r_copy(d):
        at_row = pl.ds(pl.multiple_of(r * w_rows, w_rows), w_rows)
        return remote(
            wcol, wgrad.at[at_row], r_send.at[d - 1], r_recv.at[d - 1], (b, lax.rem(r + d, replicas))
        )

    def r_arrival(d):
        source = lax.rem(r + replicas - d, replicas)
        at_row = pl.ds(pl.multiple_of(source * w_rows, w_rows), w_rows)
        return remote(wcol, wgrad.at[at_row], r_send.at[d - 1], r_recv.at[d - 1], (b, source))

    for t in range(pairs):
        gsend[t] = grad_terms(2 * t + 1).astype(gsend.dtype).reshape(gsend.shape[1:])
        for k in range(replicas):
            odd_copy(t, k).start()
    for t in range(pairs):
        gterm[t] = grad_terms(2 * t).reshape(gterm.shape[1:])

    if whole_weight:
        wpart[...] = weight_rows()
        repeat(blocks, lambda d: w_copy(d).start(), 1)
    else:
        wgrad[...] = weight_rows()

    for t in range(pairs):
        for k in range(replicas):
            send_grad(t, k)

    if whole_weight:
        repeat(blocks, lambda d: w_copy(d).wait_recv(), 1)
        chunk = wpart[chunk_of(b), :]
        for d in range(1, blocks):
            chunk = chunk + wslots[d - 1]
        wcol[chunk_of(b), :] = chunk
        repeat(blocks, lambda d: c_copy(d).start(), 1)
        repeat(blocks, lambda d: c_arrival(d).wait_recv(), 1)
        repeat(replicas, lambda d: r_copy(d).start(), 1)
        wgrad[pl.ds(pl.multiple_of(r * w_rows, w_rows), w_rows), :] = wcol[...]

    def grad_arrival(j):
        copy = remote(
            gslots.at[j], gslots.at[j], g_send.at[0, 0], g_recv.at[j], (blk_at(-2 * j), j // pairs)
        )

        @pl.when(jnp.logical_or(j != 0, r != 0))
        def _():
            copy.wait_recv()

    repeat(blocks // 2, grad_arrival)
    summed = gslots[0].astype(jnp.float32)
    for j in range(1, blocks // 2):
        summed = summed + gslots[j].astype(jnp.float32)
    fgrad[...] = summed.astype(jnp.bfloat16)

    for t in range(pairs):
        for c, h in pieces:
            hand_copy(t, c, h).wait_send()
    repeat(replicas, lambda d: dz_copy(d).wait_send(), 1)
    repeat(replicas, lambda d: agg_copy(d).wait_send(), 1)
    for t in range(pairs):
        for k in range(replicas):
            odd_copy(t, k).wait_send()
            if t == 0 and k == 0:

                @pl.when(r != 0)
                def _():
                    grad_copy(t, k).wait_send()
            else:
                grad_copy(t, k).wait_send()
    if whole_weight:
        repeat(blocks, lambda d: w_copy(d).wait_send(), 1)
        repeat(blocks, lambda d: c_copy(d).wait_send(), 1)
        repeat(replicas, lambda d: r_arrival(d).wait_recv(), 1)
        repeat(replicas, lambda d: r_copy(d).wait_send(), 1)


def per_device(features, weight, cotangent, tile_values, tile_rows, tile_cols, tile_count):
    rows_blk, width = features.shape
    sections, slots = tile_rows.shape[1:]
    replicas = lax.axis_size("rep")
    blocks = lax.axis_size("blk")
    nodes = rows_blk * blocks
    own_rows = rows_blk // replicas
    w_rows = width // replicas
    w_chunk = w_rows // blocks if w_rows % (8 * blocks) == 0 else 0
    dims = (blocks, replicas, sections, rows_blk, width, slots, own_rows, w_rows, w_chunk, nodes)
    bf16, f32 = jnp.bfloat16, jnp.float32
    vmem = pl.BlockSpec(memory_space=pltpu.VMEM)
    dma = pltpu.SemaphoreType.DMA
    others = max(replicas - 1, 1)
    pairs, parts = sections // 2, width // TILE
    act, wgrad, fgrad = pl.pallas_call(
        functools.partial(kernel, dims),
        out_shape=(
            jax.ShapeDtypeStruct((own_rows, width), bf16),
            jax.ShapeDtypeStruct((width if w_chunk else w_rows, width), f32),
            jax.ShapeDtypeStruct((own_rows, width), bf16),
        ),
        in_specs=[pl.BlockSpec(memory_space=pltpu.HBM)] * 7,
        out_specs=(vmem, vmem, vmem),
        scratch_shapes=[
            pltpu.VMEM(weight.shape, bf16),
            pltpu.VMEM(cotangent.shape, bf16),
            pltpu.VMEM(tile_values.shape, bf16),
            pltpu.SMEM(tile_rows.shape, jnp.int32),
            pltpu.SMEM(tile_cols.shape, jnp.int32),
            pltpu.SMEM(tile_count.shape, jnp.int32),
            pltpu.VMEM((sections, parts, rows_blk, TILE), bf16),
            pltpu.VMEM((rows_blk, sections * rows_blk), bf16),
            pltpu.VMEM((sections * rows_blk, rows_blk), bf16),
            pltpu.VMEM((parts, rows_blk, TILE), bf16),
            pltpu.VMEM((others, parts, own_rows, TILE), bf16),
            pltpu.VMEM((rows_blk, width), bf16),
            pltpu.VMEM((width, own_rows), bf16),
            pltpu.VMEM((replicas, w_rows, own_rows), bf16),
            pltpu.VMEM((pairs, replicas, own_rows, width), bf16),
            pltpu.VMEM((pairs, replicas, own_rows, width), bf16),
            pltpu.VMEM((pairs, replicas, own_rows, width), bf16),
            pltpu.VMEM((blocks // 2, own_rows, width), bf16),
            pltpu.VMEM((w_rows, width), f32),
            pltpu.VMEM((blocks, max(w_chunk, 8), width), f32),
            pltpu.VMEM((w_rows, width), f32),
            pltpu.VMEM((rows_blk, TILE), f32),
            pltpu.VMEM(weight.shape, bf16),
            pltpu.VMEM((pairs, replicas, own_rows, width), f32),
            dma((6,)),
            dma((pairs, parts, HALVES)),
            dma((pairs, parts, HALVES)),
            dma((pairs, parts, HALVES)),
            dma((pairs, parts, HALVES)),
            dma((others, parts)),
            dma((others, parts)),
            dma((others,)),
            dma((others,)),
            dma((others,)),
            dma((others,)),
            dma((pairs, replicas)),
            dma((pairs, replicas)),
            dma((pairs, replicas)),
            dma((blocks // 2,)),
            dma((blocks,)),
            dma((blocks,)),
            dma((blocks,)),
            dma((blocks,)),
            dma((others,)),
            dma((others,)),
        ],
        compiler_params=pltpu.CompilerParams(
            collective_id=0, has_side_effects=True, vmem_limit_bytes=48 * 1024 * 1024
        ),
        name="graph_layer",
    )(features, weight, cotangent, tile_values, tile_rows, tile_cols, tile_count)
    if not w_chunk:
        wgrad = lax.all_gather(lax.psum(wgrad, "blk"), "rep", axis=0, tiled=True)
    return (act, wgrad, fgrad)


def solution(mesh):
    return jax.shard_map(
        per_device,
        mesh=mesh,
        in_specs=(
            P("blk", None),
            P(),
            P(("blk", "rep"), None),
            P("blk", "rep", None, None, None),
            P("blk", "rep", None),
            P("blk", "rep", None),
            P("blk", "rep"),
        ),
        out_specs=(P(("blk", "rep"), None), P(), P(("blk", "rep"), None)),
        check_vma=False,
    )
```

```python
import functools
import math

import jax
import jax.numpy as jnp
from jax import lax
from jax.experimental import pallas as pl
from jax.experimental.pallas import tpu as pltpu
from jax.sharding import PartitionSpec as P

MESH = pl.DeviceIdType.MESH
TILE = 128
UNROLL = 8
HALVES = 2


def repeat(count, body, first=0):
    if count - first <= UNROLL:
        for index in range(first, count):
            body(index)
    else:

        def step(index, carry):
            body(index)
            return carry

        lax.fori_loop(first, count, step, 0)


def kernel(dims, *refs):
    blocks, replicas, sections, rows_blk, width, slots, own_rows, w_rows, w_chunk, nodes = dims
    (feat, weight_hbm, cot_hbm, tiles_hbm, trows_hbm, tcols_hbm, tcount_hbm) = refs[:7]
    (act, wgrad, fgrad) = refs[7:10]
    (weight, cot, tiles, trows, tcols, tcount) = refs[10:16]
    (fbuf, amat, amat_t, pbuf, rbuf, dzfull, agg_t, aggs) = refs[16:24]
    (gsend, gpair, gbuf, gslots, wpart, wslots, wcol) = refs[24:31]
    (pfull, weight_t, gterm, wmine, wall, l_sem) = refs[31:37]
    (f_send, f_recv, h_send, h_recv, p_send, p_recv, z_send, z_recv, a_send, a_recv) = refs[37:47]
    (o_send, o_recv, g_send, g_recv, w_send, w_recv, c_send, c_recv, r_send, r_recv) = refs[47:]
    b = lax.axis_index("blk")
    r = lax.axis_index("rep")
    odd = lax.rem(b, 2)
    pairs = sections // 2
    row_tiles = rows_blk // TILE
    column_parts = width // TILE
    whole_weight = w_chunk > 0
    pieces = [(c, h) for c in range(column_parts) for h in range(HALVES)]

    def blk_at(offset):
        return lax.rem(b + offset + 2 * blocks, blocks)

    def remote(src, dst, send, recv, to):
        return pltpu.make_async_remote_copy(
            src_ref=src, dst_ref=dst, send_sem=send, recv_sem=recv, device_id=to, device_id_type=MESH
        )

    local = [
        pltpu.make_async_copy(src, dst, l_sem.at[n])
        for n, (src, dst) in enumerate(
            (
                (trows_hbm, trows),
                (tcols_hbm, tcols),
                (tcount_hbm, tcount),
                (tiles_hbm, tiles),
                (weight_hbm, weight),
                (cot_hbm, cot),
            )
        )
    ]
    for copy in local:
        copy.start()

    barrier = pltpu.get_barrier_semaphore()

    def greet(to):
        pl.semaphore_signal(barrier, inc=1, device_id=to, device_id_type=MESH)

    neighbour = b + 1 - 2 * odd
    repeat(replicas, lambda d: greet((b, lax.rem(r + d, replicas))), 1)
    repeat(blocks, lambda d: greet((blk_at(d), r)), 1)
    greet((neighbour, lax.rem(r + 2 * odd - 1 + replicas, replicas)))

    def greet_grad(j):
        @pl.when(jnp.logical_or(j != 0, r != 0))
        def _():
            greet((blk_at(-2 * j), 2 * j // sections))

    repeat(blocks // 2, greet_grad)
    own = jnp.where(r == 0, 1, 0)
    pl.semaphore_wait(barrier, replicas + blocks - 1 + pairs * replicas - own)

    half_rows = rows_blk // HALVES

    def piece(section, c, h):
        return fbuf.at[section, c, pl.ds(h * half_rows, half_rows)]

    def feature_piece(c, h):
        return feat.at[pl.ds(h * half_rows, half_rows), pl.ds(c * TILE, TILE)]

    def feature_copy(t, c, h):
        return remote(
            feature_piece(c, h),
            piece(2 * t, c, h),
            f_send.at[t, c, h],
            f_recv.at[t, c, h],
            (blk_at(-(sections * r + 2 * t)), r),
        )

    def feature_local(c, h):
        return pltpu.make_async_copy(feature_piece(c, h), piece(0, c, h), f_recv.at[0, c, h])

    def hand_copy(t, c, h):
        section = lax.rem(2 * t + 2 * odd - 1 + sections, sections)
        back = jnp.where(odd == 0, 1, 0) if t == 0 else 0
        return remote(
            piece(2 * t, c, h),
            piece(section, c, h),
            h_send.at[t, c, h],
            h_recv.at[section // 2, c, h],
            (neighbour, lax.rem(r - back + replicas, replicas)),
        )

    def hand_arrival(t, c, h):
        here = piece(2 * t + 1, c, h)
        return remote(here, here, h_send.at[t, c, h], h_recv.at[t, c, h], (neighbour, r))

    for c, h in pieces:
        for t in range(pairs):
            if t == 0:

                @pl.when(r != 0)
                def _():
                    feature_copy(0, c, h).start()

                @pl.when(r == 0)
                def _():
                    feature_local(c, h).start()
            else:
                feature_copy(t, c, h).start()

    for copy in local[:4]:
        copy.wait()

    def place_tiles(s):
        count = tcount[0, s]
        place = [
            jnp.where(t < count, trows[0, s, t] * row_tiles + tcols[0, s, t], -1)
            for t in range(slots)
        ]
        for i in range(row_tiles):
            for j in range(row_tiles):
                slot = jnp.int32(0)
                for t in range(slots):
                    slot = jnp.where(place[t] == i * row_tiles + j, t + 1, slot)
                tile = tiles[0, s, jnp.maximum(slot - 1, 0)]
                tile = jnp.where(slot > 0, tile, jnp.zeros_like(tile))
                at_col = pl.ds(s * rows_blk + j * TILE, TILE)
                amat[pl.ds(i * TILE, TILE), at_col] = tile

    def turn_tiles(s):
        for i in range(row_tiles):
            for j in range(row_tiles):
                at_row = pl.ds(i * TILE, TILE)
                at_col = pl.ds(s * rows_blk + j * TILE, TILE)
                amat_t[at_col, at_row] = amat[at_row, at_col].T

    for s in range(pairs):
        place_tiles(s)
    for n, (c, h) in enumerate(pieces):
        for t in range(pairs):
            if t == 0:

                @pl.when(r != 0)
                def _():
                    feature_copy(0, c, h).wait()

                @pl.when(r == 0)
                def _():
                    feature_local(c, h).wait()
            else:
                feature_copy(t, c, h).wait()
            hand_copy(t, c, h).start()
        if n == 0:
            for s in range(pairs, sections):
                place_tiles(s)

    def rows_of(k):
        return pl.ds(pl.multiple_of(k * own_rows, own_rows), own_rows)

    def partial_copy(d, c):
        peer = lax.rem(r + d, replicas)
        return remote(
            pbuf.at[c, rows_of(peer)],
            rbuf.at[d - 1, c],
            p_send.at[d - 1, c],
            p_recv.at[d - 1, c],
            (b, peer),
        )

    totals = []
    for c in range(column_parts):
        for h in range(HALVES):
            for t in range(pairs):
                hand_arrival(t, c, h).wait_recv()
        product = jnp.zeros((rows_blk, TILE), jnp.float32)
        for s in range(sections):
            product = product + jnp.dot(
                amat[:, s * rows_blk : (s + 1) * rows_blk],
                fbuf[s, c],
                preferred_element_type=jnp.float32,
            )
        pbuf[c] = product.astype(pbuf.dtype)
        repeat(replicas, lambda d: partial_copy(d, c).start(), 1)
        pfull[...] = product
        totals.append(pfull[rows_of(r), :])
    for s in range(1, sections, 2):
        turn_tiles(s)
    for copy in local[4:]:
        copy.wait()
    weight_t[...] = weight[...].T
    for c in range(column_parts):
        repeat(replicas, lambda d: partial_copy(d, c).wait(), 1)
        for d in range(1, replicas):
            totals[c] = totals[c] + rbuf[d - 1, c].astype(jnp.float32)
    agg = jnp.concatenate(totals, axis=1).astype(jnp.bfloat16)

    z_value = jnp.dot(agg, weight[...], preferred_element_type=jnp.float32)
    sigma = jax.nn.sigmoid(z_value)
    dz = (cot[...].astype(jnp.float32) * sigma * (1.0 + z_value * (1.0 - sigma))).astype(jnp.bfloat16)
    mine = pl.ds(pl.multiple_of(r * own_rows, own_rows), own_rows)
    dzfull[mine, :] = dz

    def dz_copy(d):
        return remote(
            dzfull.at[mine],
            dzfull.at[mine],
            z_send.at[d - 1],
            z_recv.at[d - 1],
            (b, lax.rem(r + d, replicas)),
        )

    def dz_arrival(d):
        source = lax.rem(r + replicas - d, replicas)
        at_row = pl.ds(pl.multiple_of(source * own_rows, own_rows), own_rows)
        return remote(
            dzfull.at[at_row], dzfull.at[at_row], z_send.at[d - 1], z_recv.at[d - 1], (b, source)
        )

    repeat(replicas, lambda d: dz_copy(d).start(), 1)
    agg_t[...] = agg.T

    def agg_copy(d):
        peer = lax.rem(r + d, replicas)
        at_row = pl.ds(pl.multiple_of(peer * w_rows, w_rows), w_rows)
        return remote(agg_t.at[at_row], aggs.at[d], a_send.at[d - 1], a_recv.at[d - 1], (b, peer))

    repeat(replicas, lambda d: agg_copy(d).start(), 1)
    aggs[0] = agg_t[pl.ds(pl.multiple_of(r * w_rows, w_rows), w_rows), :]
    act[...] = (z_value * sigma).astype(jnp.bfloat16)
    for s in range(0, sections, 2):
        turn_tiles(s)

    repeat(replicas, lambda d: dz_arrival(d).wait_recv(), 1)
    dy = jnp.dot(dzfull[...], weight_t[...], preferred_element_type=jnp.float32).astype(jnp.bfloat16)

    def grad_terms(s):
        at_row = pl.ds(s * rows_blk, rows_blk)
        return jnp.dot(amat_t[at_row, :], dy, preferred_element_type=jnp.float32)

    def odd_copy(t, k):
        slot = lax.rem(t + odd, pairs)
        ahead = odd if t == pairs - 1 else 0
        return remote(
            gsend.at[t, k],
            gpair.at[slot, k],
            o_send.at[t, k],
            o_recv.at[slot, k],
            (neighbour, lax.rem(r + ahead, replicas)),
        )

    def odd_arrival(t, k):
        here = gpair.at[t, k]
        return remote(here, here, o_send.at[t, k], o_recv.at[t, k], (neighbour, r))

    def grad_copy(t, k):
        j = pairs * r + t
        return remote(
            gbuf.at[t, k], gslots.at[j], g_send.at[t, k], g_recv.at[j], (blk_at(2 * j), k)
        )

    def send_grad(t, k):
        term = gterm[t, k]
        odd_arrival(t, k).wait_recv()
        gbuf[t, k] = (term + gpair[t, k].astype(jnp.float32)).astype(gbuf.dtype)
        if t == 0 and k == 0:

            @pl.when(r != 0)
            def _():
                grad_copy(t, k).start()

            @pl.when(r == 0)
            def _():
                gslots[0] = gbuf[0, 0]
        else:
            grad_copy(t, k).start()

    def weight_rows():
        repeat(replicas, lambda d: agg_copy(d).wait_recv(), 1)
        acc = jnp.zeros((w_rows, width), jnp.float32)
        for d in range(replicas):
            source = lax.rem(r + replicas - d, replicas)
            at_row = pl.ds(pl.multiple_of(source * own_rows, own_rows), own_rows)
            acc = acc + jnp.dot(aggs[d], dzfull[at_row, :], preferred_element_type=jnp.float32)
        return acc * (1.0 / math.sqrt(nodes))

    def chunk_of(at):
        return pl.ds(pl.multiple_of(at * w_chunk, w_chunk), w_chunk)

    def w_copy(d):
        return remote(
            wpart.at[chunk_of(blk_at(d))], wslots.at[d - 1], w_send.at[d - 1], w_recv.at[d - 1], (blk_at(d), r)
        )

    def c_copy(d):
        return remote(
            wcol.at[chunk_of(b)], wcol.at[chunk_of(b)], c_send.at[d - 1], c_recv.at[d - 1], (blk_at(d), r)
        )

    def c_arrival(d):
        at_row = chunk_of(blk_at(-d))
        return remote(wcol.at[at_row], wcol.at[at_row], c_send.at[d - 1], c_recv.at[d - 1], (blk_at(-d), r))

    def r_copy(d):
        at_row = pl.ds(pl.multiple_of(r * w_rows, w_rows), w_rows)
        return remote(
            wmine, wall.at[at_row], r_send.at[d - 1], r_recv.at[d - 1], (b, lax.rem(r + d, replicas))
        )

    def r_arrival(d):
        source = lax.rem(r + replicas - d, replicas)
        at_row = pl.ds(pl.multiple_of(source * w_rows, w_rows), w_rows)
        return remote(wmine, wall.at[at_row], r_send.at[d - 1], r_recv.at[d - 1], (b, source))

    def weight_sum():
        repeat(blocks, lambda d: w_copy(d).wait_recv(), 1)
        chunk = wpart[chunk_of(b), :]
        for d in range(1, blocks):
            chunk = chunk + wslots[d - 1]
        wcol[chunk_of(b), :] = chunk
        repeat(blocks, lambda d: c_copy(d).start(), 1)

    def weight_gather():
        repeat(blocks, lambda d: c_arrival(d).wait_recv(), 1)
        wmine[...] = wcol[...].astype(wmine.dtype)
        repeat(replicas, lambda d: r_copy(d).start(), 1)

    odd_first = grad_terms(1).astype(gsend.dtype).reshape(gsend.shape[1:])
    gsend[0] = odd_first
    for k in range(replicas):
        odd_copy(0, k).start()
    if whole_weight:
        wpart[...] = weight_rows()
        repeat(blocks, lambda d: w_copy(d).start(), 1)
    else:
        wgrad[...] = weight_rows()
    for t in range(1, pairs):
        gsend[t] = grad_terms(2 * t + 1).astype(gsend.dtype).reshape(gsend.shape[1:])
        for k in range(replicas):
            odd_copy(t, k).start()
    for t in range(pairs):
        gterm[t] = grad_terms(2 * t).reshape(gterm.shape[1:])

    for t in range(pairs):
        for k in range(replicas):
            send_grad(t, k)
            if whole_weight and t == 0 and k == 0:
                weight_sum()
            if whole_weight and t == pairs - 1 and k == max(replicas - 2, 0):
                weight_gather()

    def grad_arrival(j):
        copy = remote(
            gslots.at[j], gslots.at[j], g_send.at[0, 0], g_recv.at[j], (blk_at(-2 * j), j // pairs)
        )

        @pl.when(jnp.logical_or(j != 0, r != 0))
        def _():
            copy.wait_recv()

    repeat(blocks // 2, grad_arrival)
    summed = gslots[0].astype(jnp.float32)
    for j in range(1, blocks // 2):
        summed = summed + gslots[j].astype(jnp.float32)
    fgrad[...] = summed.astype(jnp.bfloat16)

    if whole_weight:
        at_row = pl.ds(pl.multiple_of(r * w_rows, w_rows), w_rows)
        wall[at_row, :] = wmine[...]
        repeat(replicas, lambda d: r_arrival(d).wait_recv(), 1)
        wgrad[...] = wall[...].astype(jnp.float32)

    for t in range(pairs):
        for c, h in pieces:
            hand_copy(t, c, h).wait_send()
    repeat(replicas, lambda d: dz_copy(d).wait_send(), 1)
    repeat(replicas, lambda d: agg_copy(d).wait_send(), 1)
    for t in range(pairs):
        for k in range(replicas):
            odd_copy(t, k).wait_send()
            if t == 0 and k == 0:

                @pl.when(r != 0)
                def _():
                    grad_copy(t, k).wait_send()
            else:
                grad_copy(t, k).wait_send()
    if whole_weight:
        repeat(blocks, lambda d: w_copy(d).wait_send(), 1)
        repeat(blocks, lambda d: c_copy(d).wait_send(), 1)
        repeat(replicas, lambda d: r_copy(d).wait_send(), 1)


def per_device(features, weight, cotangent, tile_values, tile_rows, tile_cols, tile_count):
    rows_blk, width = features.shape
    sections, slots = tile_rows.shape[1:]
    replicas = lax.axis_size("rep")
    blocks = lax.axis_size("blk")
    nodes = rows_blk * blocks
    own_rows = rows_blk // replicas
    w_rows = width // replicas
    w_chunk = w_rows // blocks if w_rows % (8 * blocks) == 0 else 0
    dims = (blocks, replicas, sections, rows_blk, width, slots, own_rows, w_rows, w_chunk, nodes)
    bf16, f32 = jnp.bfloat16, jnp.float32
    vmem = pl.BlockSpec(memory_space=pltpu.VMEM)
    dma = pltpu.SemaphoreType.DMA
    others = max(replicas - 1, 1)
    pairs, parts = sections // 2, width // TILE
    act, wgrad, fgrad = pl.pallas_call(
        functools.partial(kernel, dims),
        out_shape=(
            jax.ShapeDtypeStruct((own_rows, width), bf16),
            jax.ShapeDtypeStruct((width if w_chunk else w_rows, width), f32),
            jax.ShapeDtypeStruct((own_rows, width), bf16),
        ),
        in_specs=[pl.BlockSpec(memory_space=pltpu.HBM)] * 7,
        out_specs=(vmem, vmem, vmem),
        scratch_shapes=[
            pltpu.VMEM(weight.shape, bf16),
            pltpu.VMEM(cotangent.shape, bf16),
            pltpu.VMEM(tile_values.shape, bf16),
            pltpu.SMEM(tile_rows.shape, jnp.int32),
            pltpu.SMEM(tile_cols.shape, jnp.int32),
            pltpu.SMEM(tile_count.shape, jnp.int32),
            pltpu.VMEM((sections, parts, rows_blk, TILE), bf16),
            pltpu.VMEM((rows_blk, sections * rows_blk), bf16),
            pltpu.VMEM((sections * rows_blk, rows_blk), bf16),
            pltpu.VMEM((parts, rows_blk, TILE), bf16),
            pltpu.VMEM((others, parts, own_rows, TILE), bf16),
            pltpu.VMEM((rows_blk, width), bf16),
            pltpu.VMEM((width, own_rows), bf16),
            pltpu.VMEM((replicas, w_rows, own_rows), bf16),
            pltpu.VMEM((pairs, replicas, own_rows, width), bf16),
            pltpu.VMEM((pairs, replicas, own_rows, width), bf16),
            pltpu.VMEM((pairs, replicas, own_rows, width), bf16),
            pltpu.VMEM((blocks // 2, own_rows, width), bf16),
            pltpu.VMEM((w_rows, width), f32),
            pltpu.VMEM((blocks, max(w_chunk, 8), width), f32),
            pltpu.VMEM((w_rows, width), f32),
            pltpu.VMEM((rows_blk, TILE), f32),
            pltpu.VMEM(weight.shape, bf16),
            pltpu.VMEM((pairs, replicas, own_rows, width), f32),
            pltpu.VMEM((w_rows, width), bf16),
            pltpu.VMEM((width, width), bf16),
            dma((6,)),
            dma((pairs, parts, HALVES)),
            dma((pairs, parts, HALVES)),
            dma((pairs, parts, HALVES)),
            dma((pairs, parts, HALVES)),
            dma((others, parts)),
            dma((others, parts)),
            dma((others,)),
            dma((others,)),
            dma((others,)),
            dma((others,)),
            dma((pairs, replicas)),
            dma((pairs, replicas)),
            dma((pairs, replicas)),
            dma((blocks // 2,)),
            dma((blocks,)),
            dma((blocks,)),
            dma((blocks,)),
            dma((blocks,)),
            dma((others,)),
            dma((others,)),
        ],
        compiler_params=pltpu.CompilerParams(
            collective_id=0, has_side_effects=True
        ),
        name="graph_layer",
    )(features, weight, cotangent, tile_values, tile_rows, tile_cols, tile_count)
    if not w_chunk:
        wgrad = lax.all_gather(lax.psum(wgrad, "blk"), "rep", axis=0, tiled=True)
    return (act, wgrad, fgrad)


def solution(mesh):
    return jax.shard_map(
        per_device,
        mesh=mesh,
        in_specs=(
            P("blk", None),
            P(),
            P(("blk", "rep"), None),
            P("blk", "rep", None, None, None),
            P("blk", "rep", None),
            P("blk", "rep", None),
            P("blk", "rep"),
        ),
        out_specs=(P(("blk", "rep"), None), P(), P(("blk", "rep"), None)),
        check_vma=False,
    )
```

```python
import functools
import math

import jax
import jax.numpy as jnp
from jax import lax
from jax.experimental import pallas as pl
from jax.experimental.pallas import tpu as pltpu
from jax.sharding import PartitionSpec as P

MESH = pl.DeviceIdType.MESH
TILE = 128
UNROLL = 8
HALVES = 2


def repeat(count, body, first=0):
    if count - first <= UNROLL:
        for index in range(first, count):
            body(index)
    else:

        def step(index, carry):
            body(index)
            return carry

        lax.fori_loop(first, count, step, 0)


def kernel(dims, *refs):
    blocks, replicas, sections, rows_blk, width, slots, own_rows, w_rows, w_chunk, nodes = dims
    (feat, weight_hbm, cot_hbm, tiles_hbm, trows_hbm, tcols_hbm, tcount_hbm) = refs[:7]
    (act, wgrad, fgrad) = refs[7:10]
    (weight, cot, tiles, trows, tcols, tcount) = refs[10:16]
    (fbuf, amat, amat_t, pbuf, rbuf, dzfull, agg_t, aggs) = refs[16:24]
    (gsend, gpair, gbuf, gslots, wpart, wslots, wcol) = refs[24:31]
    (pfull, weight_t, gterm, wmine, wall, xbuf) = refs[31:37]
    (x_send, x_recv, v_send, l_sem) = refs[37:41]
    (f_send, f_recv, h_send, h_recv, p_send, p_recv, z_send, z_recv, a_send, a_recv) = refs[41:51]
    (o_send, o_recv, g_send, g_recv, w_send, w_recv, c_send, c_recv, r_send, r_recv) = refs[51:]
    b = lax.axis_index("blk")
    r = lax.axis_index("rep")
    odd = lax.rem(b, 2)
    pairs = sections // 2
    row_tiles = rows_blk // TILE
    column_parts = width // TILE
    whole_weight = w_chunk > 0
    detour = replicas == 4 and sections == 2
    pieces = [(c, h) for c in range(column_parts) for h in range(HALVES)]

    def blk_at(offset):
        return lax.rem(b + offset + 2 * blocks, blocks)

    def remote(src, dst, send, recv, to):
        return pltpu.make_async_remote_copy(
            src_ref=src, dst_ref=dst, send_sem=send, recv_sem=recv, device_id=to, device_id_type=MESH
        )

    local = [
        pltpu.make_async_copy(src, dst, l_sem.at[n])
        for n, (src, dst) in enumerate(
            (
                (trows_hbm, trows),
                (tcols_hbm, tcols),
                (tcount_hbm, tcount),
                (tiles_hbm, tiles),
                (weight_hbm, weight),
                (cot_hbm, cot),
            )
        )
    ]
    for copy in local:
        copy.start()

    barrier = pltpu.get_barrier_semaphore()

    def greet(to):
        pl.semaphore_signal(barrier, inc=1, device_id=to, device_id_type=MESH)

    neighbour = b + 1 - 2 * odd
    repeat(replicas, lambda d: greet((b, lax.rem(r + d, replicas))), 1)
    repeat(blocks, lambda d: greet((blk_at(d), r)), 1)
    greet((neighbour, lax.rem(r + 2 * odd - 1 + replicas, replicas)))

    def greet_grad(j):
        @pl.when(jnp.logical_or(j != 0, r != 0))
        def _():
            greet((blk_at(-2 * j), 2 * j // sections))

    repeat(blocks // 2, greet_grad)
    own = jnp.where(r == 0, 1, 0)
    pl.semaphore_wait(barrier, replicas + blocks - 1 + pairs * replicas - own)

    half_rows = rows_blk // HALVES

    def piece(section, c, h):
        return fbuf.at[section, c, pl.ds(h * half_rows, half_rows)]

    def feature_piece(c, h):
        return feat.at[pl.ds(h * half_rows, half_rows), pl.ds(c * TILE, TILE)]

    def feature_copy(t, c, h):
        return remote(
            feature_piece(c, h),
            piece(2 * t, c, h),
            f_send.at[t, c, h],
            f_recv.at[t, c, h],
            (blk_at(-(sections * r + 2 * t)), r),
        )

    def feature_local(c, h):
        return pltpu.make_async_copy(feature_piece(c, h), piece(0, c, h), f_recv.at[0, c, h])

    def hand_copy(t, c, h):
        section = lax.rem(2 * t + 2 * odd - 1 + sections, sections)
        back = jnp.where(odd == 0, 1, 0) if t == 0 else 0
        return remote(
            piece(2 * t, c, h),
            piece(section, c, h),
            h_send.at[t, c, h],
            h_recv.at[section // 2, c, h],
            (neighbour, lax.rem(r - back + replicas, replicas)),
        )

    def hand_arrival(t, c, h):
        here = piece(2 * t + 1, c, h)
        return remote(here, here, h_send.at[t, c, h], h_recv.at[t, c, h], (neighbour, r))

    def detour_copy(c):
        return remote(
            feature_piece(c, HALVES - 1),
            xbuf.at[c],
            x_send.at[c],
            x_recv.at[c],
            (blk_at(-2 * sections), 0),
        )

    def detour_hand(c):
        return remote(
            xbuf.at[c], piece(0, c, HALVES - 1), v_send.at[c], f_recv.at[0, c, HALVES - 1], (b, 2)
        )

    if detour:

        @pl.when(r == 0)
        def _():
            for c in range(column_parts):
                detour_copy(c).start()

    def detoured(t, h):
        return detour and t == 0 and h == HALVES - 1

    for c, h in pieces:
        for t in range(pairs):
            if t == 0:

                @pl.when(jnp.logical_and(r != 0, r != 2) if detoured(t, h) else r != 0)
                def _():
                    feature_copy(0, c, h).start()

                @pl.when(r == 0)
                def _():
                    feature_local(c, h).start()
            else:
                feature_copy(t, c, h).start()

    for copy in local[:4]:
        copy.wait()

    def place_tiles(s):
        count = tcount[0, s]
        place = [
            jnp.where(t < count, trows[0, s, t] * row_tiles + tcols[0, s, t], -1)
            for t in range(slots)
        ]
        for i in range(row_tiles):
            for j in range(row_tiles):
                slot = jnp.int32(0)
                for t in range(slots):
                    slot = jnp.where(place[t] == i * row_tiles + j, t + 1, slot)
                tile = tiles[0, s, jnp.maximum(slot - 1, 0)]
                tile = jnp.where(slot > 0, tile, jnp.zeros_like(tile))
                at_col = pl.ds(s * rows_blk + j * TILE, TILE)
                amat[pl.ds(i * TILE, TILE), at_col] = tile

    def turn_tiles(s):
        for i in range(row_tiles):
            for j in range(row_tiles):
                at_row = pl.ds(i * TILE, TILE)
                at_col = pl.ds(s * rows_blk + j * TILE, TILE)
                amat_t[at_col, at_row] = amat[at_row, at_col].T

    for s in range(pairs):
        place_tiles(s)
    for n, (c, h) in enumerate(pieces):
        for t in range(pairs):
            if t == 0:

                @pl.when(jnp.logical_and(r != 0, r != 2) if detoured(t, h) else r != 0)
                def _():
                    feature_copy(0, c, h).wait_send()

                @pl.when(r != 0)
                def _():
                    feature_copy(0, c, h).wait_recv()

                @pl.when(r == 0)
                def _():
                    feature_local(c, h).wait()
            else:
                feature_copy(t, c, h).wait()
            hand_copy(t, c, h).start()
        if n == 0:
            for s in range(pairs, sections):
                place_tiles(s)

    if detour:

        @pl.when(r == 0)
        def _():
            for c in range(column_parts):
                detour_copy(c).wait_recv()
                detour_hand(c).start()

    def rows_of(k):
        return pl.ds(pl.multiple_of(k * own_rows, own_rows), own_rows)

    def partial_copy(d, c):
        peer = lax.rem(r + d, replicas)
        return remote(
            pbuf.at[c, rows_of(peer)],
            rbuf.at[d - 1, c],
            p_send.at[d - 1, c],
            p_recv.at[d - 1, c],
            (b, peer),
        )

    totals = []
    for c in range(column_parts):
        for h in range(HALVES):
            for t in range(pairs):
                hand_arrival(t, c, h).wait_recv()
        product = jnp.zeros((rows_blk, TILE), jnp.float32)
        for s in range(sections):
            product = product + jnp.dot(
                amat[:, s * rows_blk : (s + 1) * rows_blk],
                fbuf[s, c],
                preferred_element_type=jnp.float32,
            )
        pbuf[c] = product.astype(pbuf.dtype)
        repeat(replicas, lambda d: partial_copy(d, c).start(), 1)
        pfull[...] = product
        totals.append(pfull[rows_of(r), :])
    for s in range(1, sections, 2):
        turn_tiles(s)
    for copy in local[4:]:
        copy.wait()
    weight_t[...] = weight[...].T
    for c in range(column_parts):
        repeat(replicas, lambda d: partial_copy(d, c).wait(), 1)
        for d in range(1, replicas):
            totals[c] = totals[c] + rbuf[d - 1, c].astype(jnp.float32)
    agg = jnp.concatenate(totals, axis=1).astype(jnp.bfloat16)

    z_value = jnp.dot(agg, weight[...], preferred_element_type=jnp.float32)
    sigma = jax.nn.sigmoid(z_value)
    dz = (cot[...].astype(jnp.float32) * sigma * (1.0 + z_value * (1.0 - sigma))).astype(jnp.bfloat16)
    mine = pl.ds(pl.multiple_of(r * own_rows, own_rows), own_rows)
    dzfull[mine, :] = dz

    def dz_copy(d):
        return remote(
            dzfull.at[mine],
            dzfull.at[mine],
            z_send.at[d - 1],
            z_recv.at[d - 1],
            (b, lax.rem(r + d, replicas)),
        )

    def dz_arrival(d):
        source = lax.rem(r + replicas - d, replicas)
        at_row = pl.ds(pl.multiple_of(source * own_rows, own_rows), own_rows)
        return remote(
            dzfull.at[at_row], dzfull.at[at_row], z_send.at[d - 1], z_recv.at[d - 1], (b, source)
        )

    repeat(replicas, lambda d: dz_copy(d).start(), 1)
    agg_t[...] = agg.T

    def agg_copy(d):
        peer = lax.rem(r + d, replicas)
        at_row = pl.ds(pl.multiple_of(peer * w_rows, w_rows), w_rows)
        return remote(agg_t.at[at_row], aggs.at[d], a_send.at[d - 1], a_recv.at[d - 1], (b, peer))

    repeat(replicas, lambda d: agg_copy(d).start(), 1)
    aggs[0] = agg_t[pl.ds(pl.multiple_of(r * w_rows, w_rows), w_rows), :]
    act[...] = (z_value * sigma).astype(jnp.bfloat16)
    for s in range(0, sections, 2):
        turn_tiles(s)

    repeat(replicas, lambda d: dz_arrival(d).wait_recv(), 1)
    dy = jnp.dot(dzfull[...], weight_t[...], preferred_element_type=jnp.float32).astype(jnp.bfloat16)

    def grad_terms(s):
        at_row = pl.ds(s * rows_blk, rows_blk)
        return jnp.dot(amat_t[at_row, :], dy, preferred_element_type=jnp.float32)

    def odd_copy(t, k):
        slot = lax.rem(t + odd, pairs)
        ahead = odd if t == pairs - 1 else 0
        return remote(
            gsend.at[t, k],
            gpair.at[slot, k],
            o_send.at[t, k],
            o_recv.at[slot, k],
            (neighbour, lax.rem(r + ahead, replicas)),
        )

    def odd_arrival(t, k):
        here = gpair.at[t, k]
        return remote(here, here, o_send.at[t, k], o_recv.at[t, k], (neighbour, r))

    def grad_copy(t, k):
        j = pairs * r + t
        return remote(
            gbuf.at[t, k], gslots.at[j], g_send.at[t, k], g_recv.at[j], (blk_at(2 * j), k)
        )

    def send_grad(t, k):
        term = gterm[t, k]
        odd_arrival(t, k).wait_recv()
        gbuf[t, k] = (term + gpair[t, k].astype(jnp.float32)).astype(gbuf.dtype)
        if t == 0 and k == 0:

            @pl.when(r != 0)
            def _():
                grad_copy(t, k).start()

            @pl.when(r == 0)
            def _():
                gslots[0] = gbuf[0, 0]
        else:
            grad_copy(t, k).start()

    def weight_rows():
        repeat(replicas, lambda d: agg_copy(d).wait_recv(), 1)
        acc = jnp.zeros((w_rows, width), jnp.float32)
        for d in range(replicas):
            source = lax.rem(r + replicas - d, replicas)
            at_row = pl.ds(pl.multiple_of(source * own_rows, own_rows), own_rows)
            acc = acc + jnp.dot(aggs[d], dzfull[at_row, :], preferred_element_type=jnp.float32)
        return acc * (1.0 / math.sqrt(nodes))

    def chunk_of(at):
        return pl.ds(pl.multiple_of(at * w_chunk, w_chunk), w_chunk)

    def w_copy(d):
        return remote(
            wpart.at[chunk_of(blk_at(d))], wslots.at[d - 1], w_send.at[d - 1], w_recv.at[d - 1], (blk_at(d), r)
        )

    def c_copy(d):
        return remote(
            wcol.at[chunk_of(b)], wcol.at[chunk_of(b)], c_send.at[d - 1], c_recv.at[d - 1], (blk_at(d), r)
        )

    def c_arrival(d):
        at_row = chunk_of(blk_at(-d))
        return remote(wcol.at[at_row], wcol.at[at_row], c_send.at[d - 1], c_recv.at[d - 1], (blk_at(-d), r))

    def r_copy(d):
        at_row = pl.ds(pl.multiple_of(r * w_rows, w_rows), w_rows)
        return remote(
            wmine, wall.at[at_row], r_send.at[d - 1], r_recv.at[d - 1], (b, lax.rem(r + d, replicas))
        )

    def r_arrival(d):
        source = lax.rem(r + replicas - d, replicas)
        at_row = pl.ds(pl.multiple_of(source * w_rows, w_rows), w_rows)
        return remote(wmine, wall.at[at_row], r_send.at[d - 1], r_recv.at[d - 1], (b, source))

    def weight_sum():
        repeat(blocks, lambda d: w_copy(d).wait_recv(), 1)
        chunk = wpart[chunk_of(b), :]
        for d in range(1, blocks):
            chunk = chunk + wslots[d - 1]
        wcol[chunk_of(b), :] = chunk
        repeat(blocks, lambda d: c_copy(d).start(), 1)

    def weight_gather():
        repeat(blocks, lambda d: c_arrival(d).wait_recv(), 1)
        wmine[...] = wcol[...].astype(wmine.dtype)
        repeat(replicas, lambda d: r_copy(d).start(), 1)

    odd_first = grad_terms(1).astype(gsend.dtype).reshape(gsend.shape[1:])
    gsend[0] = odd_first
    for k in range(replicas):
        odd_copy(0, k).start()
    if whole_weight:
        wpart[...] = weight_rows()
        repeat(blocks, lambda d: w_copy(d).start(), 1)
    else:
        wgrad[...] = weight_rows()
    for t in range(1, pairs):
        gsend[t] = grad_terms(2 * t + 1).astype(gsend.dtype).reshape(gsend.shape[1:])
        for k in range(replicas):
            odd_copy(t, k).start()
    for t in range(pairs):
        gterm[t] = grad_terms(2 * t).reshape(gterm.shape[1:])

    for t in range(pairs):
        for k in range(replicas):
            send_grad(t, k)
            if whole_weight and t == 0 and k == 0:
                weight_sum()
            if whole_weight and t == pairs - 1 and k == max(replicas - 2, 0):
                weight_gather()

    def grad_arrival(j):
        copy = remote(
            gslots.at[j], gslots.at[j], g_send.at[0, 0], g_recv.at[j], (blk_at(-2 * j), j // pairs)
        )

        @pl.when(jnp.logical_or(j != 0, r != 0))
        def _():
            copy.wait_recv()

    repeat(blocks // 2, grad_arrival)
    summed = gslots[0].astype(jnp.float32)
    for j in range(1, blocks // 2):
        summed = summed + gslots[j].astype(jnp.float32)
    fgrad[...] = summed.astype(jnp.bfloat16)

    if whole_weight:
        at_row = pl.ds(pl.multiple_of(r * w_rows, w_rows), w_rows)
        wall[at_row, :] = wmine[...]
        repeat(replicas, lambda d: r_arrival(d).wait_recv(), 1)
        wgrad[...] = wall[...].astype(jnp.float32)

    if detour:

        @pl.when(r == 0)
        def _():
            for c in range(column_parts):
                detour_copy(c).wait_send()
                detour_hand(c).wait_send()

    for t in range(pairs):
        for c, h in pieces:
            hand_copy(t, c, h).wait_send()
    repeat(replicas, lambda d: dz_copy(d).wait_send(), 1)
    repeat(replicas, lambda d: agg_copy(d).wait_send(), 1)
    for t in range(pairs):
        for k in range(replicas):
            odd_copy(t, k).wait_send()
            if t == 0 and k == 0:

                @pl.when(r != 0)
                def _():
                    grad_copy(t, k).wait_send()
            else:
                grad_copy(t, k).wait_send()
    if whole_weight:
        repeat(blocks, lambda d: w_copy(d).wait_send(), 1)
        repeat(blocks, lambda d: c_copy(d).wait_send(), 1)
        repeat(replicas, lambda d: r_copy(d).wait_send(), 1)


def publish(*refs):
    copies = [pltpu.make_async_copy(refs[n], refs[3 + n], refs[6].at[n]) for n in range(3)]
    for copy in copies:
        copy.start()
    for copy in copies:
        copy.wait()


def per_device(features, weight, cotangent, tile_values, tile_rows, tile_cols, tile_count):
    rows_blk, width = features.shape
    sections, slots = tile_rows.shape[1:]
    replicas = lax.axis_size("rep")
    blocks = lax.axis_size("blk")
    nodes = rows_blk * blocks
    own_rows = rows_blk // replicas
    w_rows = width // replicas
    w_chunk = w_rows // blocks if w_rows % (8 * blocks) == 0 else 0
    dims = (blocks, replicas, sections, rows_blk, width, slots, own_rows, w_rows, w_chunk, nodes)
    bf16, f32 = jnp.bfloat16, jnp.float32
    vmem = pl.BlockSpec(memory_space=pltpu.VMEM)
    dma = pltpu.SemaphoreType.DMA
    others = max(replicas - 1, 1)
    pairs, parts = sections // 2, width // TILE
    act, wgrad, fgrad = pl.pallas_call(
        functools.partial(kernel, dims),
        out_shape=(
            jax.ShapeDtypeStruct((own_rows, width), bf16),
            jax.ShapeDtypeStruct((width if w_chunk else w_rows, width), f32),
            jax.ShapeDtypeStruct((own_rows, width), bf16),
        ),
        in_specs=[pl.BlockSpec(memory_space=pltpu.HBM)] * 7,
        out_specs=(vmem, vmem, vmem),
        scratch_shapes=[
            pltpu.VMEM(weight.shape, bf16),
            pltpu.VMEM(cotangent.shape, bf16),
            pltpu.VMEM(tile_values.shape, bf16),
            pltpu.SMEM(tile_rows.shape, jnp.int32),
            pltpu.SMEM(tile_cols.shape, jnp.int32),
            pltpu.SMEM(tile_count.shape, jnp.int32),
            pltpu.VMEM((sections, parts, rows_blk, TILE), bf16),
            pltpu.VMEM((rows_blk, sections * rows_blk), bf16),
            pltpu.VMEM((sections * rows_blk, rows_blk), bf16),
            pltpu.VMEM((parts, rows_blk, TILE), bf16),
            pltpu.VMEM((others, parts, own_rows, TILE), bf16),
            pltpu.VMEM((rows_blk, width), bf16),
            pltpu.VMEM((width, own_rows), bf16),
            pltpu.VMEM((replicas, w_rows, own_rows), bf16),
            pltpu.VMEM((pairs, replicas, own_rows, width), bf16),
            pltpu.VMEM((pairs, replicas, own_rows, width), bf16),
            pltpu.VMEM((pairs, replicas, own_rows, width), bf16),
            pltpu.VMEM((blocks // 2, own_rows, width), bf16),
            pltpu.VMEM((w_rows, width), f32),
            pltpu.VMEM((blocks, max(w_chunk, 8), width), f32),
            pltpu.VMEM((w_rows, width), f32),
            pltpu.VMEM((rows_blk, TILE), f32),
            pltpu.VMEM(weight.shape, bf16),
            pltpu.VMEM((pairs, replicas, own_rows, width), f32),
            pltpu.VMEM((w_rows, width), bf16),
            pltpu.VMEM((width, width), bf16),
            pltpu.VMEM((parts, rows_blk // HALVES, TILE), bf16),
            dma((parts,)),
            dma((parts,)),
            dma((parts,)),
            dma((6,)),
            dma((pairs, parts, HALVES)),
            dma((pairs, parts, HALVES)),
            dma((pairs, parts, HALVES)),
            dma((pairs, parts, HALVES)),
            dma((others, parts)),
            dma((others, parts)),
            dma((others,)),
            dma((others,)),
            dma((others,)),
            dma((others,)),
            dma((pairs, replicas)),
            dma((pairs, replicas)),
            dma((pairs, replicas)),
            dma((blocks // 2,)),
            dma((blocks,)),
            dma((blocks,)),
            dma((blocks,)),
            dma((blocks,)),
            dma((others,)),
            dma((others,)),
        ],
        compiler_params=pltpu.CompilerParams(
            collective_id=0, has_side_effects=True
        ),
        name="graph_layer",
    )(features, weight, cotangent, tile_values, tile_rows, tile_cols, tile_count)
    if not w_chunk:
        wgrad = lax.all_gather(lax.psum(wgrad, "blk"), "rep", axis=0, tiled=True)
    results = (act, wgrad, fgrad)
    return pl.pallas_call(
        publish,
        out_shape=tuple(jax.ShapeDtypeStruct(x.shape, x.dtype) for x in results),
        in_specs=[pl.BlockSpec(memory_space=pl.ANY)] * 3,
        out_specs=(pl.BlockSpec(memory_space=pl.ANY),) * 3,
        scratch_shapes=[dma((3,))],
        name="publish",
    )(*results)


def solution(mesh):
    return jax.shard_map(
        per_device,
        mesh=mesh,
        in_specs=(
            P("blk", None),
            P(),
            P(("blk", "rep"), None),
            P("blk", "rep", None, None, None),
            P("blk", "rep", None),
            P("blk", "rep", None),
            P("blk", "rep"),
        ),
        out_specs=(P(("blk", "rep"), None), P(), P(("blk", "rep"), None)),
        check_vma=False,
    )
```

```python
import functools
import math

import jax
import jax.numpy as jnp
from jax import lax
from jax.experimental import pallas as pl
from jax.experimental.pallas import tpu as pltpu
from jax.sharding import PartitionSpec as P

MESH = pl.DeviceIdType.MESH
TILE = 128
UNROLL = 8
HALVES = 2


def repeat(count, body, first=0):
    if count - first <= UNROLL:
        for index in range(first, count):
            body(index)
    else:

        def step(index, carry):
            body(index)
            return carry

        lax.fori_loop(first, count, step, 0)


def kernel(dims, *refs):
    blocks, replicas, sections, rows_blk, width, slots, own_rows, w_rows, w_chunk, nodes = dims
    (feat, weight_hbm, cot_hbm, tiles_hbm, trows_hbm, tcols_hbm, tcount_hbm) = refs[:7]
    (act, wgrad, fgrad) = refs[7:10]
    (weight, cot, tiles, trows, tcols, tcount) = refs[10:16]
    (fbuf, amat, amat_t, pbuf, rbuf, dzfull, agg_t, aggs) = refs[16:24]
    (gsend, gpair, gbuf, gslots, wpart, wslots, wcol) = refs[24:31]
    (pfull, weight_t, gterm, wmine, wall, fown) = refs[31:37]
    (s_sem, l_sem) = refs[37:39]
    (f_send, f_recv, h_send, h_recv, p_send, p_recv, z_send, z_recv, a_send, a_recv) = refs[39:49]
    (o_send, o_recv, g_send, g_recv, w_send, w_recv, c_send, c_recv, r_send, r_recv) = refs[49:]
    b = lax.axis_index("blk")
    r = lax.axis_index("rep")
    odd = lax.rem(b, 2)
    pairs = sections // 2
    row_tiles = rows_blk // TILE
    column_parts = width // TILE
    whole_weight = w_chunk > 0
    pieces = [(c, h) for c in range(column_parts) for h in range(HALVES)]

    def blk_at(offset):
        return lax.rem(b + offset + 2 * blocks, blocks)

    def remote(src, dst, send, recv, to):
        return pltpu.make_async_remote_copy(
            src_ref=src, dst_ref=dst, send_sem=send, recv_sem=recv, device_id=to, device_id_type=MESH
        )

    local = [
        pltpu.make_async_copy(src, dst, l_sem.at[n])
        for n, (src, dst) in enumerate(
            (
                (trows_hbm, trows),
                (tcols_hbm, tcols),
                (tcount_hbm, tcount),
                (tiles_hbm, tiles),
                (weight_hbm, weight),
                (cot_hbm, cot),
            )
        )
    ]
    loads = [
        pltpu.make_async_copy(feat.at[:, pl.ds(c * TILE, TILE)], fown.at[c], s_sem.at[c])
        for c in range(column_parts)
    ]
    for copy in loads + local:
        copy.start()

    barrier = pltpu.get_barrier_semaphore()

    def greet(to):
        pl.semaphore_signal(barrier, inc=1, device_id=to, device_id_type=MESH)

    neighbour = b + 1 - 2 * odd
    repeat(replicas, lambda d: greet((b, lax.rem(r + d, replicas))), 1)
    repeat(blocks, lambda d: greet((blk_at(d), r)), 1)
    greet((neighbour, lax.rem(r + 2 * odd - 1 + replicas, replicas)))

    def greet_grad(j):
        @pl.when(jnp.logical_or(j != 0, r != 0))
        def _():
            greet((blk_at(-2 * j), 2 * j // sections))

    repeat(blocks // 2, greet_grad)
    own = jnp.where(r == 0, 1, 0)
    pl.semaphore_wait(barrier, replicas + blocks - 1 + pairs * replicas - own)

    half_rows = rows_blk // HALVES

    def piece(section, c, h):
        return fbuf.at[section, c, pl.ds(h * half_rows, half_rows)]

    def feature_piece(c, h):
        return fown.at[c, pl.ds(h * half_rows, half_rows)]

    def feature_copy(t, c, h):
        return remote(
            feature_piece(c, h),
            piece(2 * t, c, h),
            f_send.at[t, c, h],
            f_recv.at[t, c, h],
            (blk_at(-(sections * r + 2 * t)), r),
        )

    def feature_local(c, h):
        return pltpu.make_async_copy(feature_piece(c, h), piece(0, c, h), f_recv.at[0, c, h])

    def hand_copy(t, c, h):
        section = lax.rem(2 * t + 2 * odd - 1 + sections, sections)
        back = jnp.where(odd == 0, 1, 0) if t == 0 else 0
        return remote(
            piece(2 * t, c, h),
            piece(section, c, h),
            h_send.at[t, c, h],
            h_recv.at[section // 2, c, h],
            (neighbour, lax.rem(r - back + replicas, replicas)),
        )

    def hand_arrival(t, c, h):
        here = piece(2 * t + 1, c, h)
        return remote(here, here, h_send.at[t, c, h], h_recv.at[t, c, h], (neighbour, r))

    for c, h in pieces:
        if h == 0:
            loads[c].wait()
        for t in range(pairs):
            if t == 0:

                @pl.when(r != 0)
                def _():
                    feature_copy(0, c, h).start()

                @pl.when(r == 0)
                def _():
                    feature_local(c, h).start()
            else:
                feature_copy(t, c, h).start()

    for copy in local[:4]:
        copy.wait()

    def place_tiles(s):
        count = tcount[0, s]
        place = [
            jnp.where(t < count, trows[0, s, t] * row_tiles + tcols[0, s, t], -1)
            for t in range(slots)
        ]
        for i in range(row_tiles):
            for j in range(row_tiles):
                slot = jnp.int32(0)
                for t in range(slots):
                    slot = jnp.where(place[t] == i * row_tiles + j, t + 1, slot)
                tile = tiles[0, s, jnp.maximum(slot - 1, 0)]
                tile = jnp.where(slot > 0, tile, jnp.zeros_like(tile))
                at_col = pl.ds(s * rows_blk + j * TILE, TILE)
                amat[pl.ds(i * TILE, TILE), at_col] = tile

    def turn_tiles(s):
        for i in range(row_tiles):
            for j in range(row_tiles):
                at_row = pl.ds(i * TILE, TILE)
                at_col = pl.ds(s * rows_blk + j * TILE, TILE)
                amat_t[at_col, at_row] = amat[at_row, at_col].T

    for s in range(pairs):
        place_tiles(s)
    for n, (c, h) in enumerate(pieces):
        for t in range(pairs):
            if t == 0:

                @pl.when(r != 0)
                def _():
                    feature_copy(0, c, h).wait()

                @pl.when(r == 0)
                def _():
                    feature_local(c, h).wait()
            else:
                feature_copy(t, c, h).wait()
            hand_copy(t, c, h).start()
        if n == 0:
            for s in range(pairs, sections):
                place_tiles(s)

    def rows_of(k):
        return pl.ds(pl.multiple_of(k * own_rows, own_rows), own_rows)

    def partial_copy(d, c):
        peer = lax.rem(r + d, replicas)
        return remote(
            pbuf.at[c, rows_of(peer)],
            rbuf.at[d - 1, c],
            p_send.at[d - 1, c],
            p_recv.at[d - 1, c],
            (b, peer),
        )

    totals = []
    for c in range(column_parts):
        for h in range(HALVES):
            for t in range(pairs):
                hand_arrival(t, c, h).wait_recv()
        product = jnp.zeros((rows_blk, TILE), jnp.float32)
        for s in range(sections):
            product = product + jnp.dot(
                amat[:, s * rows_blk : (s + 1) * rows_blk],
                fbuf[s, c],
                preferred_element_type=jnp.float32,
            )
        pbuf[c] = product.astype(pbuf.dtype)
        repeat(replicas, lambda d: partial_copy(d, c).start(), 1)
        pfull[...] = product
        totals.append(pfull[rows_of(r), :])
    for s in range(1, sections, 2):
        turn_tiles(s)
    for copy in local[4:]:
        copy.wait()
    weight_t[...] = weight[...].T
    for c in range(column_parts):
        repeat(replicas, lambda d: partial_copy(d, c).wait(), 1)
        for d in range(1, replicas):
            totals[c] = totals[c] + rbuf[d - 1, c].astype(jnp.float32)
    agg = jnp.concatenate(totals, axis=1).astype(jnp.bfloat16)

    z_value = jnp.dot(agg, weight[...], preferred_element_type=jnp.float32)
    sigma = jax.nn.sigmoid(z_value)
    dz = (cot[...].astype(jnp.float32) * sigma * (1.0 + z_value * (1.0 - sigma))).astype(jnp.bfloat16)
    mine = pl.ds(pl.multiple_of(r * own_rows, own_rows), own_rows)
    dzfull[mine, :] = dz

    def dz_copy(d):
        return remote(
            dzfull.at[mine],
            dzfull.at[mine],
            z_send.at[d - 1],
            z_recv.at[d - 1],
            (b, lax.rem(r + d, replicas)),
        )

    def dz_arrival(d):
        source = lax.rem(r + replicas - d, replicas)
        at_row = pl.ds(pl.multiple_of(source * own_rows, own_rows), own_rows)
        return remote(
            dzfull.at[at_row], dzfull.at[at_row], z_send.at[d - 1], z_recv.at[d - 1], (b, source)
        )

    repeat(replicas, lambda d: dz_copy(d).start(), 1)
    agg_t[...] = agg.T

    def agg_copy(d):
        peer = lax.rem(r + d, replicas)
        at_row = pl.ds(pl.multiple_of(peer * w_rows, w_rows), w_rows)
        return remote(agg_t.at[at_row], aggs.at[d], a_send.at[d - 1], a_recv.at[d - 1], (b, peer))

    repeat(replicas, lambda d: agg_copy(d).start(), 1)
    aggs[0] = agg_t[pl.ds(pl.multiple_of(r * w_rows, w_rows), w_rows), :]
    act[...] = (z_value * sigma).astype(jnp.bfloat16)
    for s in range(0, sections, 2):
        turn_tiles(s)

    repeat(replicas, lambda d: dz_arrival(d).wait_recv(), 1)
    dy = jnp.dot(dzfull[...], weight_t[...], preferred_element_type=jnp.float32).astype(jnp.bfloat16)

    def grad_terms(s):
        at_row = pl.ds(s * rows_blk, rows_blk)
        return jnp.dot(amat_t[at_row, :], dy, preferred_element_type=jnp.float32)

    def odd_copy(t, k):
        slot = lax.rem(t + odd, pairs)
        ahead = odd if t == pairs - 1 else 0
        return remote(
            gsend.at[t, k],
            gpair.at[slot, k],
            o_send.at[t, k],
            o_recv.at[slot, k],
            (neighbour, lax.rem(r + ahead, replicas)),
        )

    def odd_arrival(t, k):
        here = gpair.at[t, k]
        return remote(here, here, o_send.at[t, k], o_recv.at[t, k], (neighbour, r))

    def grad_copy(t, k):
        j = pairs * r + t
        return remote(
            gbuf.at[t, k], gslots.at[j], g_send.at[t, k], g_recv.at[j], (blk_at(2 * j), k)
        )

    def send_grad(t, k):
        term = gterm[t, k]
        odd_arrival(t, k).wait_recv()
        gbuf[t, k] = (term + gpair[t, k].astype(jnp.float32)).astype(gbuf.dtype)
        if t == 0 and k == 0:

            @pl.when(r != 0)
            def _():
                grad_copy(t, k).start()

            @pl.when(r == 0)
            def _():
                gslots[0] = gbuf[0, 0]
        else:
            grad_copy(t, k).start()

    def weight_rows():
        repeat(replicas, lambda d: agg_copy(d).wait_recv(), 1)
        acc = jnp.zeros((w_rows, width), jnp.float32)
        for d in range(replicas):
            source = lax.rem(r + replicas - d, replicas)
            at_row = pl.ds(pl.multiple_of(source * own_rows, own_rows), own_rows)
            acc = acc + jnp.dot(aggs[d], dzfull[at_row, :], preferred_element_type=jnp.float32)
        return acc * (1.0 / math.sqrt(nodes))

    def chunk_of(at):
        return pl.ds(pl.multiple_of(at * w_chunk, w_chunk), w_chunk)

    def w_copy(d):
        return remote(
            wpart.at[chunk_of(blk_at(d))], wslots.at[d - 1], w_send.at[d - 1], w_recv.at[d - 1], (blk_at(d), r)
        )

    def c_copy(d):
        return remote(
            wcol.at[chunk_of(b)], wcol.at[chunk_of(b)], c_send.at[d - 1], c_recv.at[d - 1], (blk_at(d), r)
        )

    def c_arrival(d):
        at_row = chunk_of(blk_at(-d))
        return remote(wcol.at[at_row], wcol.at[at_row], c_send.at[d - 1], c_recv.at[d - 1], (blk_at(-d), r))

    def r_copy(d):
        at_row = pl.ds(pl.multiple_of(r * w_rows, w_rows), w_rows)
        return remote(
            wmine, wall.at[at_row], r_send.at[d - 1], r_recv.at[d - 1], (b, lax.rem(r + d, replicas))
        )

    def r_arrival(d):
        source = lax.rem(r + replicas - d, replicas)
        at_row = pl.ds(pl.multiple_of(source * w_rows, w_rows), w_rows)
        return remote(wmine, wall.at[at_row], r_send.at[d - 1], r_recv.at[d - 1], (b, source))

    def weight_sum():
        repeat(blocks, lambda d: w_copy(d).wait_recv(), 1)
        chunk = wpart[chunk_of(b), :]
        for d in range(1, blocks):
            chunk = chunk + wslots[d - 1]
        wcol[chunk_of(b), :] = chunk
        repeat(blocks, lambda d: c_copy(d).start(), 1)

    def weight_gather():
        repeat(blocks, lambda d: c_arrival(d).wait_recv(), 1)
        wmine[...] = wcol[...].astype(wmine.dtype)
        repeat(replicas, lambda d: r_copy(d).start(), 1)

    odd_first = grad_terms(1).astype(gsend.dtype).reshape(gsend.shape[1:])
    gsend[0] = odd_first
    for k in range(replicas):
        odd_copy(0, k).start()
    if whole_weight:
        wpart[...] = weight_rows()
        repeat(blocks, lambda d: w_copy(d).start(), 1)
    else:
        wgrad[...] = weight_rows()
    for t in range(1, pairs):
        gsend[t] = grad_terms(2 * t + 1).astype(gsend.dtype).reshape(gsend.shape[1:])
        for k in range(replicas):
            odd_copy(t, k).start()
    for t in range(pairs):
        gterm[t] = grad_terms(2 * t).reshape(gterm.shape[1:])

    for t in range(pairs):
        for k in range(replicas):
            send_grad(t, k)
            if whole_weight and t == 0 and k == 0:
                weight_sum()
            if whole_weight and t == pairs - 1 and k == max(replicas - 2, 0):
                weight_gather()

    def grad_arrival(j):
        copy = remote(
            gslots.at[j], gslots.at[j], g_send.at[0, 0], g_recv.at[j], (blk_at(-2 * j), j // pairs)
        )

        @pl.when(jnp.logical_or(j != 0, r != 0))
        def _():
            copy.wait_recv()

    repeat(blocks // 2, grad_arrival)
    summed = gslots[0].astype(jnp.float32)
    for j in range(1, blocks // 2):
        summed = summed + gslots[j].astype(jnp.float32)
    fgrad[...] = summed.astype(jnp.bfloat16)

    if whole_weight:
        at_row = pl.ds(pl.multiple_of(r * w_rows, w_rows), w_rows)
        wall[at_row, :] = wmine[...]
        repeat(replicas, lambda d: r_arrival(d).wait_recv(), 1)
        wgrad[...] = wall[...].astype(jnp.float32)

    for t in range(pairs):
        for c, h in pieces:
            hand_copy(t, c, h).wait_send()
    repeat(replicas, lambda d: dz_copy(d).wait_send(), 1)
    repeat(replicas, lambda d: agg_copy(d).wait_send(), 1)
    for t in range(pairs):
        for k in range(replicas):
            odd_copy(t, k).wait_send()
            if t == 0 and k == 0:

                @pl.when(r != 0)
                def _():
                    grad_copy(t, k).wait_send()
            else:
                grad_copy(t, k).wait_send()
    if whole_weight:
        repeat(blocks, lambda d: w_copy(d).wait_send(), 1)
        repeat(blocks, lambda d: c_copy(d).wait_send(), 1)
        repeat(replicas, lambda d: r_copy(d).wait_send(), 1)


def publish(*refs):
    for n in range(3):
        refs[3 + n][...] = refs[n][...]


def per_device(features, weight, cotangent, tile_values, tile_rows, tile_cols, tile_count):
    rows_blk, width = features.shape
    sections, slots = tile_rows.shape[1:]
    replicas = lax.axis_size("rep")
    blocks = lax.axis_size("blk")
    nodes = rows_blk * blocks
    own_rows = rows_blk // replicas
    w_rows = width // replicas
    w_chunk = w_rows // blocks if w_rows % (8 * blocks) == 0 else 0
    dims = (blocks, replicas, sections, rows_blk, width, slots, own_rows, w_rows, w_chunk, nodes)
    bf16, f32 = jnp.bfloat16, jnp.float32
    vmem = pl.BlockSpec(memory_space=pltpu.VMEM)
    dma = pltpu.SemaphoreType.DMA
    others = max(replicas - 1, 1)
    pairs, parts = sections // 2, width // TILE
    act, wgrad, fgrad = pl.pallas_call(
        functools.partial(kernel, dims),
        out_shape=(
            jax.ShapeDtypeStruct((own_rows, width), bf16),
            jax.ShapeDtypeStruct((width if w_chunk else w_rows, width), f32),
            jax.ShapeDtypeStruct((own_rows, width), bf16),
        ),
        in_specs=[pl.BlockSpec(memory_space=pltpu.HBM)] * 7,
        out_specs=(vmem, vmem, vmem),
        scratch_shapes=[
            pltpu.VMEM(weight.shape, bf16),
            pltpu.VMEM(cotangent.shape, bf16),
            pltpu.VMEM(tile_values.shape, bf16),
            pltpu.SMEM(tile_rows.shape, jnp.int32),
            pltpu.SMEM(tile_cols.shape, jnp.int32),
            pltpu.SMEM(tile_count.shape, jnp.int32),
            pltpu.VMEM((sections, parts, rows_blk, TILE), bf16),
            pltpu.VMEM((rows_blk, sections * rows_blk), bf16),
            pltpu.VMEM((sections * rows_blk, rows_blk), bf16),
            pltpu.VMEM((parts, rows_blk, TILE), bf16),
            pltpu.VMEM((others, parts, own_rows, TILE), bf16),
            pltpu.VMEM((rows_blk, width), bf16),
            pltpu.VMEM((width, own_rows), bf16),
            pltpu.VMEM((replicas, w_rows, own_rows), bf16),
            pltpu.VMEM((pairs, replicas, own_rows, width), bf16),
            pltpu.VMEM((pairs, replicas, own_rows, width), bf16),
            pltpu.VMEM((pairs, replicas, own_rows, width), bf16),
            pltpu.VMEM((blocks // 2, own_rows, width), bf16),
            pltpu.VMEM((w_rows, width), f32),
            pltpu.VMEM((blocks, max(w_chunk, 8), width), f32),
            pltpu.VMEM((w_rows, width), f32),
            pltpu.VMEM((rows_blk, TILE), f32),
            pltpu.VMEM(weight.shape, bf16),
            pltpu.VMEM((pairs, replicas, own_rows, width), f32),
            pltpu.VMEM((w_rows, width), bf16),
            pltpu.VMEM((width, width), bf16),
            pltpu.VMEM((parts, rows_blk, TILE), bf16),
            dma((parts,)),
            dma((6,)),
            dma((pairs, parts, HALVES)),
            dma((pairs, parts, HALVES)),
            dma((pairs, parts, HALVES)),
            dma((pairs, parts, HALVES)),
            dma((others, parts)),
            dma((others, parts)),
            dma((others,)),
            dma((others,)),
            dma((others,)),
            dma((others,)),
            dma((pairs, replicas)),
            dma((pairs, replicas)),
            dma((pairs, replicas)),
            dma((blocks // 2,)),
            dma((blocks,)),
            dma((blocks,)),
            dma((blocks,)),
            dma((blocks,)),
            dma((others,)),
            dma((others,)),
        ],
        compiler_params=pltpu.CompilerParams(
            collective_id=0, has_side_effects=True
        ),
        name="graph_layer",
    )(features, weight, cotangent, tile_values, tile_rows, tile_cols, tile_count)
    if not w_chunk:
        wgrad = lax.all_gather(lax.psum(wgrad, "blk"), "rep", axis=0, tiled=True)
    results = (act, wgrad, fgrad)
    return pl.pallas_call(
        publish,
        out_shape=tuple(jax.ShapeDtypeStruct(x.shape, x.dtype) for x in results),
        in_specs=[vmem] * 3,
        out_specs=(vmem,) * 3,
        name="publish",
    )(*results)


def solution(mesh):
    return jax.shard_map(
        per_device,
        mesh=mesh,
        in_specs=(
            P("blk", None),
            P(),
            P(("blk", "rep"), None),
            P("blk", "rep", None, None, None),
            P("blk", "rep", None),
            P("blk", "rep", None),
            P("blk", "rep"),
        ),
        out_specs=(P(("blk", "rep"), None), P(), P(("blk", "rep"), None)),
        check_vma=False,
    )
```

```python
import functools
import math

import jax
import jax.numpy as jnp
from jax import lax
from jax.experimental import pallas as pl
from jax.experimental.pallas import tpu as pltpu
from jax.sharding import PartitionSpec as P

MESH = pl.DeviceIdType.MESH
TILE = 128
UNROLL = 8
HALVES = 2


def repeat(count, body, first=0):
    if count - first <= UNROLL:
        for index in range(first, count):
            body(index)
    else:

        def step(index, carry):
            body(index)
            return carry

        lax.fori_loop(first, count, step, 0)


def kernel(dims, *refs):
    blocks, replicas, sections, rows_blk, width, slots, own_rows, w_rows, w_chunk, nodes = dims
    (feat, weight_hbm, cot_hbm, tiles_hbm, trows_hbm, tcols_hbm, tcount_hbm) = refs[:7]
    (act, wgrad, fgrad) = refs[7:10]
    (weight, cot, tiles, trows, tcols, tcount) = refs[10:16]
    (fbuf, amat, amat_t, pbuf, rbuf, dzfull, agg_t, aggs) = refs[16:24]
    (gsend, gpair, gbuf, gslots, wpart, wslots, wcol) = refs[24:31]
    (pfull, weight_t, gterm, wmine, wall, fown) = refs[31:37]
    (s_sem, l_sem) = refs[37:39]
    (f_send, f_recv, h_send, h_recv, p_send, p_recv, z_send, z_recv, a_send, a_recv) = refs[39:49]
    (o_send, o_recv, g_send, g_recv, w_send, w_recv, c_send, c_recv, r_send, r_recv) = refs[49:]
    b = lax.axis_index("blk")
    r = lax.axis_index("rep")
    odd = lax.rem(b, 2)
    pairs = sections // 2
    row_tiles = rows_blk // TILE
    column_parts = width // TILE
    whole_weight = w_chunk > 0
    pieces = [(c, h) for c in range(column_parts) for h in range(HALVES)]

    def blk_at(offset):
        return lax.rem(b + offset + 2 * blocks, blocks)

    def remote(src, dst, send, recv, to):
        return pltpu.make_async_remote_copy(
            src_ref=src, dst_ref=dst, send_sem=send, recv_sem=recv, device_id=to, device_id_type=MESH
        )

    local = [
        pltpu.make_async_copy(src, dst, l_sem.at[n])
        for n, (src, dst) in enumerate(
            (
                (trows_hbm, trows),
                (tcols_hbm, tcols),
                (tcount_hbm, tcount),
                (tiles_hbm, tiles),
                (weight_hbm, weight),
                (cot_hbm, cot),
            )
        )
    ]
    loads = [
        pltpu.make_async_copy(feat.at[:, pl.ds(c * TILE, TILE)], fown.at[c], s_sem.at[c])
        for c in range(column_parts)
    ]
    for copy in loads + local:
        copy.start()

    barrier = pltpu.get_barrier_semaphore()

    def greet(to):
        pl.semaphore_signal(barrier, inc=1, device_id=to, device_id_type=MESH)

    neighbour = b + 1 - 2 * odd
    repeat(replicas, lambda d: greet((b, lax.rem(r + d, replicas))), 1)
    repeat(blocks, lambda d: greet((blk_at(d), r)), 1)
    greet((neighbour, lax.rem(r + 2 * odd - 1 + replicas, replicas)))

    def greet_grad(j):
        @pl.when(jnp.logical_or(j != 0, r != 0))
        def _():
            greet((blk_at(-2 * j), 2 * j // sections))

    repeat(blocks // 2, greet_grad)
    own = jnp.where(r == 0, 1, 0)
    pl.semaphore_wait(barrier, replicas + blocks - 1 + pairs * replicas - own)

    half_rows = rows_blk // HALVES

    def piece(section, c, h):
        return fbuf.at[section, c, pl.ds(h * half_rows, half_rows)]

    def feature_piece(c, h):
        return fown.at[c, pl.ds(h * half_rows, half_rows)]

    def feature_copy(t, c, h):
        return remote(
            feature_piece(c, h),
            piece(2 * t, c, h),
            f_send.at[t, c, h],
            f_recv.at[t, c, h],
            (blk_at(-(sections * r + 2 * t)), r),
        )

    def feature_local(c, h):
        return pltpu.make_async_copy(feature_piece(c, h), piece(0, c, h), f_recv.at[0, c, h])

    def hand_copy(t, c, h):
        section = lax.rem(2 * t + 2 * odd - 1 + sections, sections)
        back = jnp.where(odd == 0, 1, 0) if t == 0 else 0
        return remote(
            piece(2 * t, c, h),
            piece(section, c, h),
            h_send.at[t, c, h],
            h_recv.at[section // 2, c, h],
            (neighbour, lax.rem(r - back + replicas, replicas)),
        )

    def hand_arrival(t, c, h):
        here = piece(2 * t + 1, c, h)
        return remote(here, here, h_send.at[t, c, h], h_recv.at[t, c, h], (neighbour, r))

    for c, h in pieces:
        if h == 0:
            loads[c].wait()
        for t in range(pairs):
            if t == 0:

                @pl.when(r != 0)
                def _():
                    feature_copy(0, c, h).start()

                @pl.when(r == 0)
                def _():
                    feature_local(c, h).start()
            else:
                feature_copy(t, c, h).start()

    for copy in local[:4]:
        copy.wait()

    def place_tiles(s):
        count = tcount[0, s]
        place = [
            jnp.where(t < count, trows[0, s, t] * row_tiles + tcols[0, s, t], -1)
            for t in range(slots)
        ]
        for i in range(row_tiles):
            for j in range(row_tiles):
                slot = jnp.int32(0)
                for t in range(slots):
                    slot = jnp.where(place[t] == i * row_tiles + j, t + 1, slot)
                tile = tiles[0, s, jnp.maximum(slot - 1, 0)]
                tile = jnp.where(slot > 0, tile, jnp.zeros_like(tile))
                at_col = pl.ds(s * rows_blk + j * TILE, TILE)
                amat[pl.ds(i * TILE, TILE), at_col] = tile

    def turn_tiles(s):
        for i in range(row_tiles):
            for j in range(row_tiles):
                at_row = pl.ds(i * TILE, TILE)
                at_col = pl.ds(s * rows_blk + j * TILE, TILE)
                amat_t[at_col, at_row] = amat[at_row, at_col].T

    for s in range(pairs):
        place_tiles(s)
    for n, (c, h) in enumerate(pieces):
        for t in range(pairs):
            if t == 0:

                @pl.when(r != 0)
                def _():
                    feature_copy(0, c, h).wait()

                @pl.when(r == 0)
                def _():
                    feature_local(c, h).wait()
            else:
                feature_copy(t, c, h).wait()
            hand_copy(t, c, h).start()
        if n == 0:
            for s in range(pairs, sections):
                place_tiles(s)
        if n == 1:
            for s in range(1, sections, 2):
                turn_tiles(s)

    def rows_of(k):
        return pl.ds(pl.multiple_of(k * own_rows, own_rows), own_rows)

    def partial_copy(d, c):
        peer = lax.rem(r + d, replicas)
        return remote(
            pbuf.at[c, rows_of(peer)],
            rbuf.at[d - 1, c],
            p_send.at[d - 1, c],
            p_recv.at[d - 1, c],
            (b, peer),
        )

    totals = []
    for c in range(column_parts):
        for h in range(HALVES):
            for t in range(pairs):
                hand_arrival(t, c, h).wait_recv()
        product = jnp.zeros((rows_blk, TILE), jnp.float32)
        for s in range(sections):
            product = product + jnp.dot(
                amat[:, s * rows_blk : (s + 1) * rows_blk],
                fbuf[s, c],
                preferred_element_type=jnp.float32,
            )
        pbuf[c] = product.astype(pbuf.dtype)
        repeat(replicas, lambda d: partial_copy(d, c).start(), 1)
        pfull[...] = product
        totals.append(pfull[rows_of(r), :])
        if c == 0:
            for s in range(0, sections, 2):
                turn_tiles(s)
    for copy in local[4:]:
        copy.wait()
    weight_t[...] = weight[...].T
    for c in range(column_parts):
        repeat(replicas, lambda d: partial_copy(d, c).wait(), 1)
        for d in range(1, replicas):
            totals[c] = totals[c] + rbuf[d - 1, c].astype(jnp.float32)
    agg = jnp.concatenate(totals, axis=1).astype(jnp.bfloat16)

    z_value = jnp.dot(agg, weight[...], preferred_element_type=jnp.float32)
    sigma = jax.nn.sigmoid(z_value)
    dz = (cot[...].astype(jnp.float32) * sigma * (1.0 + z_value * (1.0 - sigma))).astype(jnp.bfloat16)
    mine = pl.ds(pl.multiple_of(r * own_rows, own_rows), own_rows)
    dzfull[mine, :] = dz

    def dz_copy(d):
        return remote(
            dzfull.at[mine],
            dzfull.at[mine],
            z_send.at[d - 1],
            z_recv.at[d - 1],
            (b, lax.rem(r + d, replicas)),
        )

    def dz_arrival(d):
        source = lax.rem(r + replicas - d, replicas)
        at_row = pl.ds(pl.multiple_of(source * own_rows, own_rows), own_rows)
        return remote(
            dzfull.at[at_row], dzfull.at[at_row], z_send.at[d - 1], z_recv.at[d - 1], (b, source)
        )

    repeat(replicas, lambda d: dz_copy(d).start(), 1)
    agg_t[...] = agg.T

    def agg_copy(d):
        peer = lax.rem(r + d, replicas)
        at_row = pl.ds(pl.multiple_of(peer * w_rows, w_rows), w_rows)
        return remote(agg_t.at[at_row], aggs.at[d], a_send.at[d - 1], a_recv.at[d - 1], (b, peer))

    repeat(replicas, lambda d: agg_copy(d).start(), 1)
    aggs[0] = agg_t[pl.ds(pl.multiple_of(r * w_rows, w_rows), w_rows), :]
    act[...] = (z_value * sigma).astype(jnp.bfloat16)

    repeat(replicas, lambda d: dz_arrival(d).wait_recv(), 1)
    dy = jnp.dot(dzfull[...], weight_t[...], preferred_element_type=jnp.float32).astype(jnp.bfloat16)

    def grad_terms(s):
        at_row = pl.ds(s * rows_blk, rows_blk)
        return jnp.dot(amat_t[at_row, :], dy, preferred_element_type=jnp.float32)

    def odd_copy(t, k):
        slot = lax.rem(t + odd, pairs)
        ahead = odd if t == pairs - 1 else 0
        return remote(
            gsend.at[t, k],
            gpair.at[slot, k],
            o_send.at[t, k],
            o_recv.at[slot, k],
            (neighbour, lax.rem(r + ahead, replicas)),
        )

    def odd_arrival(t, k):
        here = gpair.at[t, k]
        return remote(here, here, o_send.at[t, k], o_recv.at[t, k], (neighbour, r))

    def grad_copy(t, k):
        j = pairs * r + t
        return remote(
            gbuf.at[t, k], gslots.at[j], g_send.at[t, k], g_recv.at[j], (blk_at(2 * j), k)
        )

    def send_grad(t, k):
        term = gterm[t, k]
        odd_arrival(t, k).wait_recv()
        gbuf[t, k] = (term + gpair[t, k].astype(jnp.float32)).astype(gbuf.dtype)
        if t == 0 and k == 0:

            @pl.when(r != 0)
            def _():
                grad_copy(t, k).start()

            @pl.when(r == 0)
            def _():
                gslots[0] = gbuf[0, 0]
        else:
            grad_copy(t, k).start()

    def weight_rows():
        repeat(replicas, lambda d: agg_copy(d).wait_recv(), 1)
        acc = jnp.zeros((w_rows, width), jnp.float32)
        for d in range(replicas):
            source = lax.rem(r + replicas - d, replicas)
            at_row = pl.ds(pl.multiple_of(source * own_rows, own_rows), own_rows)
            acc = acc + jnp.dot(aggs[d], dzfull[at_row, :], preferred_element_type=jnp.float32)
        return acc * (1.0 / math.sqrt(nodes))

    def chunk_of(at):
        return pl.ds(pl.multiple_of(at * w_chunk, w_chunk), w_chunk)

    def w_copy(d):
        return remote(
            wpart.at[chunk_of(blk_at(d))], wslots.at[d - 1], w_send.at[d - 1], w_recv.at[d - 1], (blk_at(d), r)
        )

    def c_copy(d):
        return remote(
            wcol.at[chunk_of(b)], wcol.at[chunk_of(b)], c_send.at[d - 1], c_recv.at[d - 1], (blk_at(d), r)
        )

    def c_arrival(d):
        at_row = chunk_of(blk_at(-d))
        return remote(wcol.at[at_row], wcol.at[at_row], c_send.at[d - 1], c_recv.at[d - 1], (blk_at(-d), r))

    def r_copy(d):
        at_row = pl.ds(pl.multiple_of(r * w_rows, w_rows), w_rows)
        return remote(
            wmine, wall.at[at_row], r_send.at[d - 1], r_recv.at[d - 1], (b, lax.rem(r + d, replicas))
        )

    def r_arrival(d):
        source = lax.rem(r + replicas - d, replicas)
        at_row = pl.ds(pl.multiple_of(source * w_rows, w_rows), w_rows)
        return remote(wmine, wall.at[at_row], r_send.at[d - 1], r_recv.at[d - 1], (b, source))

    def weight_sum():
        repeat(blocks, lambda d: w_copy(d).wait_recv(), 1)
        chunk = wpart[chunk_of(b), :]
        for d in range(1, blocks):
            chunk = chunk + wslots[d - 1]
        wcol[chunk_of(b), :] = chunk
        repeat(blocks, lambda d: c_copy(d).start(), 1)

    def weight_gather():
        repeat(blocks, lambda d: c_arrival(d).wait_recv(), 1)
        wmine[...] = wcol[...].astype(wmine.dtype)
        repeat(replicas, lambda d: r_copy(d).start(), 1)

    odd_first = grad_terms(1).astype(gsend.dtype).reshape(gsend.shape[1:])
    gsend[0] = odd_first
    early = replicas // 2
    for k in range(early):
        odd_copy(0, k).start()
    if whole_weight:
        wpart[...] = weight_rows()
        repeat(blocks, lambda d: w_copy(d).start(), 1)
    else:
        wgrad[...] = weight_rows()
    for k in range(early, replicas):
        odd_copy(0, k).start()
    for t in range(1, pairs):
        gsend[t] = grad_terms(2 * t + 1).astype(gsend.dtype).reshape(gsend.shape[1:])
        for k in range(replicas):
            odd_copy(t, k).start()
    for t in range(pairs):
        gterm[t] = grad_terms(2 * t).reshape(gterm.shape[1:])

    for t in range(pairs):
        for k in range(replicas):
            send_grad(t, k)
            if whole_weight and t == pairs - 1 and k == early - 1:
                weight_sum()
    if whole_weight:
        weight_gather()

    def grad_arrival(j):
        copy = remote(
            gslots.at[j], gslots.at[j], g_send.at[0, 0], g_recv.at[j], (blk_at(-2 * j), j // pairs)
        )

        @pl.when(jnp.logical_or(j != 0, r != 0))
        def _():
            copy.wait_recv()

    repeat(blocks // 2, grad_arrival)
    summed = gslots[0].astype(jnp.float32)
    for j in range(1, blocks // 2):
        summed = summed + gslots[j].astype(jnp.float32)
    fgrad[...] = summed.astype(jnp.bfloat16)

    if whole_weight:
        at_row = pl.ds(pl.multiple_of(r * w_rows, w_rows), w_rows)
        wall[at_row, :] = wmine[...]
        repeat(replicas, lambda d: r_arrival(d).wait_recv(), 1)
        wgrad[...] = wall[...].astype(jnp.float32)

    for t in range(pairs):
        for c, h in pieces:
            hand_copy(t, c, h).wait_send()
    repeat(replicas, lambda d: dz_copy(d).wait_send(), 1)
    repeat(replicas, lambda d: agg_copy(d).wait_send(), 1)
    for t in range(pairs):
        for k in range(replicas):
            odd_copy(t, k).wait_send()
            if t == 0 and k == 0:

                @pl.when(r != 0)
                def _():
                    grad_copy(t, k).wait_send()
            else:
                grad_copy(t, k).wait_send()
    if whole_weight:
        repeat(blocks, lambda d: w_copy(d).wait_send(), 1)
        repeat(blocks, lambda d: c_copy(d).wait_send(), 1)
        repeat(replicas, lambda d: r_copy(d).wait_send(), 1)


def publish(*refs):
    for n in range(3):
        refs[3 + n][...] = refs[n][...]


def per_device(features, weight, cotangent, tile_values, tile_rows, tile_cols, tile_count):
    rows_blk, width = features.shape
    sections, slots = tile_rows.shape[1:]
    replicas = lax.axis_size("rep")
    blocks = lax.axis_size("blk")
    nodes = rows_blk * blocks
    own_rows = rows_blk // replicas
    w_rows = width // replicas
    w_chunk = w_rows // blocks if w_rows % (8 * blocks) == 0 else 0
    dims = (blocks, replicas, sections, rows_blk, width, slots, own_rows, w_rows, w_chunk, nodes)
    bf16, f32 = jnp.bfloat16, jnp.float32
    vmem = pl.BlockSpec(memory_space=pltpu.VMEM)
    dma = pltpu.SemaphoreType.DMA
    others = max(replicas - 1, 1)
    pairs, parts = sections // 2, width // TILE
    act, wgrad, fgrad = pl.pallas_call(
        functools.partial(kernel, dims),
        out_shape=(
            jax.ShapeDtypeStruct((own_rows, width), bf16),
            jax.ShapeDtypeStruct((width if w_chunk else w_rows, width), f32),
            jax.ShapeDtypeStruct((own_rows, width), bf16),
        ),
        in_specs=[pl.BlockSpec(memory_space=pltpu.HBM)] * 7,
        out_specs=(vmem, vmem, vmem),
        scratch_shapes=[
            pltpu.VMEM(weight.shape, bf16),
            pltpu.VMEM(cotangent.shape, bf16),
            pltpu.VMEM(tile_values.shape, bf16),
            pltpu.SMEM(tile_rows.shape, jnp.int32),
            pltpu.SMEM(tile_cols.shape, jnp.int32),
            pltpu.SMEM(tile_count.shape, jnp.int32),
            pltpu.VMEM((sections, parts, rows_blk, TILE), bf16),
            pltpu.VMEM((rows_blk, sections * rows_blk), bf16),
            pltpu.VMEM((sections * rows_blk, rows_blk), bf16),
            pltpu.VMEM((parts, rows_blk, TILE), bf16),
            pltpu.VMEM((others, parts, own_rows, TILE), bf16),
            pltpu.VMEM((rows_blk, width), bf16),
            pltpu.VMEM((width, own_rows), bf16),
            pltpu.VMEM((replicas, w_rows, own_rows), bf16),
            pltpu.VMEM((pairs, replicas, own_rows, width), bf16),
            pltpu.VMEM((pairs, replicas, own_rows, width), bf16),
            pltpu.VMEM((pairs, replicas, own_rows, width), bf16),
            pltpu.VMEM((blocks // 2, own_rows, width), bf16),
            pltpu.VMEM((w_rows, width), f32),
            pltpu.VMEM((blocks, max(w_chunk, 8), width), f32),
            pltpu.VMEM((w_rows, width), f32),
            pltpu.VMEM((rows_blk, TILE), f32),
            pltpu.VMEM(weight.shape, bf16),
            pltpu.VMEM((pairs, replicas, own_rows, width), f32),
            pltpu.VMEM((w_rows, width), bf16),
            pltpu.VMEM((width, width), bf16),
            pltpu.VMEM((parts, rows_blk, TILE), bf16),
            dma((parts,)),
            dma((6,)),
            dma((pairs, parts, HALVES)),
            dma((pairs, parts, HALVES)),
            dma((pairs, parts, HALVES)),
            dma((pairs, parts, HALVES)),
            dma((others, parts)),
            dma((others, parts)),
            dma((others,)),
            dma((others,)),
            dma((others,)),
            dma((others,)),
            dma((pairs, replicas)),
            dma((pairs, replicas)),
            dma((pairs, replicas)),
            dma((blocks // 2,)),
            dma((blocks,)),
            dma((blocks,)),
            dma((blocks,)),
            dma((blocks,)),
            dma((others,)),
            dma((others,)),
        ],
        compiler_params=pltpu.CompilerParams(
            collective_id=0, has_side_effects=True
        ),
        name="graph_layer",
    )(features, weight, cotangent, tile_values, tile_rows, tile_cols, tile_count)
    if not w_chunk:
        wgrad = lax.all_gather(lax.psum(wgrad, "blk"), "rep", axis=0, tiled=True)
    results = (act, wgrad, fgrad)
    return pl.pallas_call(
        publish,
        out_shape=tuple(jax.ShapeDtypeStruct(x.shape, x.dtype) for x in results),
        in_specs=[vmem] * 3,
        out_specs=(vmem,) * 3,
        name="publish",
    )(*results)


def solution(mesh):
    return jax.shard_map(
        per_device,
        mesh=mesh,
        in_specs=(
            P("blk", None),
            P(),
            P(("blk", "rep"), None),
            P("blk", "rep", None, None, None),
            P("blk", "rep", None),
            P("blk", "rep", None),
            P("blk", "rep"),
        ),
        out_specs=(P(("blk", "rep"), None), P(), P(("blk", "rep"), None)),
        check_vma=False,
    )
```

```python
import functools
import math

import jax
import jax.numpy as jnp
from jax import lax
from jax.experimental import pallas as pl
from jax.experimental.pallas import tpu as pltpu
from jax.sharding import PartitionSpec as P

MESH = pl.DeviceIdType.MESH
TILE = 128
UNROLL = 8
HALVES = 2


def repeat(count, body, first=0):
    if count - first <= UNROLL:
        for index in range(first, count):
            body(index)
    else:

        def step(index, carry):
            body(index)
            return carry

        lax.fori_loop(first, count, step, 0)


def kernel(dims, *refs):
    blocks, replicas, sections, rows_blk, width, slots, own_rows, w_rows, w_chunk, nodes = dims
    (feat, weight_hbm, cot_hbm, tiles_hbm, trows_hbm, tcols_hbm, tcount_hbm) = refs[:7]
    (act, wgrad, fgrad) = refs[7:10]
    (weight, cot, tiles, trows, tcols, tcount) = refs[10:16]
    (fbuf, amat, amat_t, pbuf, rbuf, dzfull, agg_t, aggs) = refs[16:24]
    (gsend, gpair, gbuf, gslots, wpart, wslots, wcol) = refs[24:31]
    (pfull, weight_t, gterm, wmine, wall, fown) = refs[31:37]
    (s_sem, l_sem) = refs[37:39]
    (f_send, f_recv, h_send, h_recv, p_send, p_recv, z_send, z_recv, a_send, a_recv) = refs[39:49]
    (o_send, o_recv, g_send, g_recv, w_send, w_recv, c_send, c_recv, r_send, r_recv) = refs[49:]
    b = lax.axis_index("blk")
    r = lax.axis_index("rep")
    odd = lax.rem(b, 2)
    pairs = sections // 2
    row_tiles = rows_blk // TILE
    column_parts = width // TILE
    whole_weight = w_chunk > 0
    pieces = [(c, h) for c in range(column_parts) for h in range(HALVES)]

    def blk_at(offset):
        return lax.rem(b + offset + 2 * blocks, blocks)

    def remote(src, dst, send, recv, to):
        return pltpu.make_async_remote_copy(
            src_ref=src, dst_ref=dst, send_sem=send, recv_sem=recv, device_id=to, device_id_type=MESH
        )

    local = [
        pltpu.make_async_copy(src, dst, l_sem.at[n])
        for n, (src, dst) in enumerate(
            (
                (trows_hbm, trows),
                (tcols_hbm, tcols),
                (tcount_hbm, tcount),
                (tiles_hbm, tiles),
                (weight_hbm, weight),
                (cot_hbm, cot),
            )
        )
    ]
    loads = [
        pltpu.make_async_copy(feat.at[:, pl.ds(c * TILE, TILE)], fown.at[c], s_sem.at[c])
        for c in range(column_parts)
    ]
    for copy in loads + local:
        copy.start()

    barrier = pltpu.get_barrier_semaphore()

    def greet(to):
        pl.semaphore_signal(barrier, inc=1, device_id=to, device_id_type=MESH)

    neighbour = b + 1 - 2 * odd
    repeat(replicas, lambda d: greet((b, lax.rem(r + d, replicas))), 1)
    repeat(blocks, lambda d: greet((blk_at(d), r)), 1)
    greet((neighbour, lax.rem(r + 2 * odd - 1 + replicas, replicas)))

    def greet_grad(j):
        @pl.when(jnp.logical_or(j != 0, r != 0))
        def _():
            greet((blk_at(-2 * j), 2 * j // sections))

    repeat(blocks // 2, greet_grad)
    own = jnp.where(r == 0, 1, 0)
    pl.semaphore_wait(barrier, replicas + blocks - 1 + pairs * replicas - own)

    half_rows = rows_blk // HALVES

    def piece(section, c, h):
        return fbuf.at[section, c, pl.ds(h * half_rows, half_rows)]

    def feature_piece(c, h):
        return fown.at[c, pl.ds(h * half_rows, half_rows)]

    def feature_copy(t, c, h):
        return remote(
            feature_piece(c, h),
            piece(2 * t, c, h),
            f_send.at[t, c, h],
            f_recv.at[t, c, h],
            (blk_at(-(sections * r + 2 * t)), r),
        )

    def feature_local(c, h):
        return pltpu.make_async_copy(feature_piece(c, h), piece(0, c, h), f_recv.at[0, c, h])

    def hand_copy(t, c, h):
        section = lax.rem(2 * t + 2 * odd - 1 + sections, sections)
        back = jnp.where(odd == 0, 1, 0) if t == 0 else 0
        return remote(
            piece(2 * t, c, h),
            piece(section, c, h),
            h_send.at[t, c, h],
            h_recv.at[section // 2, c, h],
            (neighbour, lax.rem(r - back + replicas, replicas)),
        )

    def hand_arrival(t, c, h):
        here = piece(2 * t + 1, c, h)
        return remote(here, here, h_send.at[t, c, h], h_recv.at[t, c, h], (neighbour, r))

    for c, h in pieces:
        if h == 0:
            loads[c].wait()
        for t in range(pairs):
            if t == 0:

                @pl.when(r != 0)
                def _():
                    feature_copy(0, c, h).start()

                @pl.when(r == 0)
                def _():
                    feature_local(c, h).start()
            else:
                feature_copy(t, c, h).start()

    for copy in local[:4]:
        copy.wait()

    def place_tiles(s):
        count = tcount[0, s]
        place = [
            jnp.where(t < count, trows[0, s, t] * row_tiles + tcols[0, s, t], -1)
            for t in range(slots)
        ]
        for i in range(row_tiles):
            for j in range(row_tiles):
                slot = jnp.int32(0)
                for t in range(slots):
                    slot = jnp.where(place[t] == i * row_tiles + j, t + 1, slot)
                tile = tiles[0, s, jnp.maximum(slot - 1, 0)]
                tile = jnp.where(slot > 0, tile, jnp.zeros_like(tile))
                at_col = pl.ds(s * rows_blk + j * TILE, TILE)
                amat[pl.ds(i * TILE, TILE), at_col] = tile

    def turn_tiles(s):
        for i in range(row_tiles):
            for j in range(row_tiles):
                at_row = pl.ds(i * TILE, TILE)
                at_col = pl.ds(s * rows_blk + j * TILE, TILE)
                amat_t[at_col, at_row] = amat[at_row, at_col].T

    for s in range(pairs):
        place_tiles(s)
    for n, (c, h) in enumerate(pieces):
        for t in range(pairs):
            if t == 0:

                @pl.when(r != 0)
                def _():
                    feature_copy(0, c, h).wait()

                @pl.when(r == 0)
                def _():
                    feature_local(c, h).wait()
            else:
                feature_copy(t, c, h).wait()
            hand_copy(t, c, h).start()
        if n == 0:
            for s in range(pairs, sections):
                place_tiles(s)
        if n == 1:
            for s in range(1, sections, 2):
                turn_tiles(s)

    def rows_of(k):
        return pl.ds(pl.multiple_of(k * own_rows, own_rows), own_rows)

    def partial_copy(d, c):
        peer = lax.rem(r + d, replicas)
        return remote(
            pbuf.at[c, rows_of(peer)],
            rbuf.at[d - 1, c],
            p_send.at[d - 1, c],
            p_recv.at[d - 1, c],
            (b, peer),
        )

    totals = []
    for c in range(column_parts):
        for h in range(HALVES):
            for t in range(pairs):
                hand_arrival(t, c, h).wait_recv()
        product = jnp.zeros((rows_blk, TILE), jnp.float32)
        for s in range(sections):
            product = product + jnp.dot(
                amat[:, s * rows_blk : (s + 1) * rows_blk],
                fbuf[s, c],
                preferred_element_type=jnp.float32,
            )
        pbuf[c] = product.astype(pbuf.dtype)
        repeat(replicas, lambda d: partial_copy(d, c).start(), 1)
        pfull[...] = product
        totals.append(pfull[rows_of(r), :])
        if c == 0:
            for s in range(0, sections, 2):
                turn_tiles(s)
    for copy in local[4:]:
        copy.wait()
    weight_t[...] = weight[...].T
    for c in range(column_parts):
        repeat(replicas, lambda d: partial_copy(d, c).wait(), 1)
        for d in range(1, replicas):
            totals[c] = totals[c] + rbuf[d - 1, c].astype(jnp.float32)
    agg = jnp.concatenate(totals, axis=1).astype(jnp.bfloat16)

    z_value = jnp.dot(agg, weight[...], preferred_element_type=jnp.float32)
    sigma = jax.nn.sigmoid(z_value)
    dz = (cot[...].astype(jnp.float32) * sigma * (1.0 + z_value * (1.0 - sigma))).astype(jnp.bfloat16)
    mine = pl.ds(pl.multiple_of(r * own_rows, own_rows), own_rows)
    dzfull[mine, :] = dz

    def dz_copy(d):
        return remote(
            dzfull.at[mine],
            dzfull.at[mine],
            z_send.at[d - 1],
            z_recv.at[d - 1],
            (b, lax.rem(r + d, replicas)),
        )

    def dz_arrival(d):
        source = lax.rem(r + replicas - d, replicas)
        at_row = pl.ds(pl.multiple_of(source * own_rows, own_rows), own_rows)
        return remote(
            dzfull.at[at_row], dzfull.at[at_row], z_send.at[d - 1], z_recv.at[d - 1], (b, source)
        )

    repeat(replicas, lambda d: dz_copy(d).start(), 1)
    agg_t[...] = agg.T

    def agg_copy(d):
        peer = lax.rem(r + d, replicas)
        at_row = pl.ds(pl.multiple_of(peer * w_rows, w_rows), w_rows)
        return remote(agg_t.at[at_row], aggs.at[d], a_send.at[d - 1], a_recv.at[d - 1], (b, peer))

    repeat(replicas, lambda d: agg_copy(d).start(), 1)
    aggs[0] = agg_t[pl.ds(pl.multiple_of(r * w_rows, w_rows), w_rows), :]
    act[...] = (z_value * sigma).astype(jnp.bfloat16)

    repeat(replicas, lambda d: dz_arrival(d).wait_recv(), 1)
    dy = jnp.dot(dzfull[...], weight_t[...], preferred_element_type=jnp.float32).astype(jnp.bfloat16)

    def grad_terms(s):
        at_row = pl.ds(s * rows_blk, rows_blk)
        return jnp.dot(amat_t[at_row, :], dy, preferred_element_type=jnp.float32)

    def odd_copy(t, k):
        slot = lax.rem(t + odd, pairs)
        ahead = odd if t == pairs - 1 else 0
        return remote(
            gsend.at[t, k],
            gpair.at[slot, k],
            o_send.at[t, k],
            o_recv.at[slot, k],
            (neighbour, lax.rem(r + ahead, replicas)),
        )

    def odd_arrival(t, k):
        here = gpair.at[t, k]
        return remote(here, here, o_send.at[t, k], o_recv.at[t, k], (neighbour, r))

    def grad_copy(t, k):
        j = pairs * r + t
        return remote(
            gbuf.at[t, k], gslots.at[j], g_send.at[t, k], g_recv.at[j], (blk_at(2 * j), k)
        )

    def send_grad(t, k):
        term = gterm[t, k]
        odd_arrival(t, k).wait_recv()
        gbuf[t, k] = (term + gpair[t, k].astype(jnp.float32)).astype(gbuf.dtype)
        if t == 0:

            @pl.when(jnp.logical_or(r != 0, k != 0))
            def _():
                grad_copy(t, k).start()

            @pl.when(jnp.logical_and(r == 0, k == 0))
            def _():
                gslots[0] = gbuf[0, 0]
        else:
            grad_copy(t, k).start()

    half = replicas // 2

    def row_order(step, rep):
        first = step // 2 + half * (step % 2)
        return lax.rem(first + half * lax.rem(rep, 2), replicas)

    def weight_rows():
        repeat(replicas, lambda d: agg_copy(d).wait_recv(), 1)
        acc = jnp.zeros((w_rows, width), jnp.float32)
        for d in range(replicas):
            source = lax.rem(r + replicas - d, replicas)
            at_row = pl.ds(pl.multiple_of(source * own_rows, own_rows), own_rows)
            acc = acc + jnp.dot(aggs[d], dzfull[at_row, :], preferred_element_type=jnp.float32)
        return acc * (1.0 / math.sqrt(nodes))

    def chunk_of(at):
        return pl.ds(pl.multiple_of(at * w_chunk, w_chunk), w_chunk)

    def w_copy(d):
        return remote(
            wpart.at[chunk_of(blk_at(d))], wslots.at[d - 1], w_send.at[d - 1], w_recv.at[d - 1], (blk_at(d), r)
        )

    def c_copy(d):
        return remote(
            wcol.at[chunk_of(b)], wcol.at[chunk_of(b)], c_send.at[d - 1], c_recv.at[d - 1], (blk_at(d), r)
        )

    def c_arrival(d):
        at_row = chunk_of(blk_at(-d))
        return remote(wcol.at[at_row], wcol.at[at_row], c_send.at[d - 1], c_recv.at[d - 1], (blk_at(-d), r))

    def r_copy(d):
        at_row = pl.ds(pl.multiple_of(r * w_rows, w_rows), w_rows)
        return remote(
            wmine, wall.at[at_row], r_send.at[d - 1], r_recv.at[d - 1], (b, lax.rem(r + d, replicas))
        )

    def r_arrival(d):
        source = lax.rem(r + replicas - d, replicas)
        at_row = pl.ds(pl.multiple_of(source * w_rows, w_rows), w_rows)
        return remote(wmine, wall.at[at_row], r_send.at[d - 1], r_recv.at[d - 1], (b, source))

    def weight_sum():
        repeat(blocks, lambda d: w_copy(d).wait_recv(), 1)
        chunk = wpart[chunk_of(b), :]
        for d in range(1, blocks):
            chunk = chunk + wslots[d - 1]
        wcol[chunk_of(b), :] = chunk
        repeat(blocks, lambda d: c_copy(d).start(), 1)

    def weight_gather():
        repeat(blocks, lambda d: c_arrival(d).wait_recv(), 1)
        wmine[...] = wcol[...].astype(wmine.dtype)
        repeat(replicas, lambda d: r_copy(d).start(), 1)

    odd_first = grad_terms(1).astype(gsend.dtype).reshape(gsend.shape[1:])
    gsend[0] = odd_first
    early = replicas // 2
    for k in range(early):
        odd_copy(0, row_order(k, r + (odd if pairs == 1 else 0))).start()
    if whole_weight:
        wpart[...] = weight_rows()
        repeat(blocks, lambda d: w_copy(d).start(), 1)
    else:
        wgrad[...] = weight_rows()
    for k in range(early, replicas):
        odd_copy(0, row_order(k, r + (odd if pairs == 1 else 0))).start()
    for t in range(1, pairs):
        gsend[t] = grad_terms(2 * t + 1).astype(gsend.dtype).reshape(gsend.shape[1:])
        for k in range(replicas):
            odd_copy(t, row_order(k, r + (odd if t == pairs - 1 else 0))).start()
    for t in range(pairs):
        gterm[t] = grad_terms(2 * t).reshape(gterm.shape[1:])

    for t in range(pairs):
        for k in range(replicas):
            send_grad(t, row_order(k, r))
            if whole_weight and t == pairs - 1 and k == early - 1:
                weight_sum()
    if whole_weight:
        weight_gather()

    def grad_arrival(j):
        copy = remote(
            gslots.at[j], gslots.at[j], g_send.at[0, 0], g_recv.at[j], (blk_at(-2 * j), j // pairs)
        )

        @pl.when(jnp.logical_or(j != 0, r != 0))
        def _():
            copy.wait_recv()

    repeat(blocks // 2, grad_arrival)
    summed = gslots[0].astype(jnp.float32)
    for j in range(1, blocks // 2):
        summed = summed + gslots[j].astype(jnp.float32)
    fgrad[...] = summed.astype(jnp.bfloat16)

    if whole_weight:
        at_row = pl.ds(pl.multiple_of(r * w_rows, w_rows), w_rows)
        wall[at_row, :] = wmine[...]
        repeat(replicas, lambda d: r_arrival(d).wait_recv(), 1)
        wgrad[...] = wall[...].astype(jnp.float32)

    for t in range(pairs):
        for c, h in pieces:
            hand_copy(t, c, h).wait_send()
    repeat(replicas, lambda d: dz_copy(d).wait_send(), 1)
    repeat(replicas, lambda d: agg_copy(d).wait_send(), 1)
    for t in range(pairs):
        for k in range(replicas):
            odd_copy(t, k).wait_send()
            if t == 0 and k == 0:

                @pl.when(r != 0)
                def _():
                    grad_copy(t, k).wait_send()
            else:
                grad_copy(t, k).wait_send()
    if whole_weight:
        repeat(blocks, lambda d: w_copy(d).wait_send(), 1)
        repeat(blocks, lambda d: c_copy(d).wait_send(), 1)
        repeat(replicas, lambda d: r_copy(d).wait_send(), 1)


def publish(*refs):
    for n in range(3):
        refs[3 + n][...] = refs[n][...]


def per_device(features, weight, cotangent, tile_values, tile_rows, tile_cols, tile_count):
    rows_blk, width = features.shape
    sections, slots = tile_rows.shape[1:]
    replicas = lax.axis_size("rep")
    blocks = lax.axis_size("blk")
    nodes = rows_blk * blocks
    own_rows = rows_blk // replicas
    w_rows = width // replicas
    w_chunk = w_rows // blocks if w_rows % (8 * blocks) == 0 else 0
    dims = (blocks, replicas, sections, rows_blk, width, slots, own_rows, w_rows, w_chunk, nodes)
    bf16, f32 = jnp.bfloat16, jnp.float32
    vmem = pl.BlockSpec(memory_space=pltpu.VMEM)
    dma = pltpu.SemaphoreType.DMA
    others = max(replicas - 1, 1)
    pairs, parts = sections // 2, width // TILE
    act, wgrad, fgrad = pl.pallas_call(
        functools.partial(kernel, dims),
        out_shape=(
            jax.ShapeDtypeStruct((own_rows, width), bf16),
            jax.ShapeDtypeStruct((width if w_chunk else w_rows, width), f32),
            jax.ShapeDtypeStruct((own_rows, width), bf16),
        ),
        in_specs=[pl.BlockSpec(memory_space=pltpu.HBM)] * 7,
        out_specs=(vmem, vmem, vmem),
        scratch_shapes=[
            pltpu.VMEM(weight.shape, bf16),
            pltpu.VMEM(cotangent.shape, bf16),
            pltpu.VMEM(tile_values.shape, bf16),
            pltpu.SMEM(tile_rows.shape, jnp.int32),
            pltpu.SMEM(tile_cols.shape, jnp.int32),
            pltpu.SMEM(tile_count.shape, jnp.int32),
            pltpu.VMEM((sections, parts, rows_blk, TILE), bf16),
            pltpu.VMEM((rows_blk, sections * rows_blk), bf16),
            pltpu.VMEM((sections * rows_blk, rows_blk), bf16),
            pltpu.VMEM((parts, rows_blk, TILE), bf16),
            pltpu.VMEM((others, parts, own_rows, TILE), bf16),
            pltpu.VMEM((rows_blk, width), bf16),
            pltpu.VMEM((width, own_rows), bf16),
            pltpu.VMEM((replicas, w_rows, own_rows), bf16),
            pltpu.VMEM((pairs, replicas, own_rows, width), bf16),
            pltpu.VMEM((pairs, replicas, own_rows, width), bf16),
            pltpu.VMEM((pairs, replicas, own_rows, width), bf16),
            pltpu.VMEM((blocks // 2, own_rows, width), bf16),
            pltpu.VMEM((w_rows, width), f32),
            pltpu.VMEM((blocks, max(w_chunk, 8), width), f32),
            pltpu.VMEM((w_rows, width), f32),
            pltpu.VMEM((rows_blk, TILE), f32),
            pltpu.VMEM(weight.shape, bf16),
            pltpu.VMEM((pairs, replicas, own_rows, width), f32),
            pltpu.VMEM((w_rows, width), bf16),
            pltpu.VMEM((width, width), bf16),
            pltpu.VMEM((parts, rows_blk, TILE), bf16),
            dma((parts,)),
            dma((6,)),
            dma((pairs, parts, HALVES)),
            dma((pairs, parts, HALVES)),
            dma((pairs, parts, HALVES)),
            dma((pairs, parts, HALVES)),
            dma((others, parts)),
            dma((others, parts)),
            dma((others,)),
            dma((others,)),
            dma((others,)),
            dma((others,)),
            dma((pairs, replicas)),
            dma((pairs, replicas)),
            dma((pairs, replicas)),
            dma((blocks // 2,)),
            dma((blocks,)),
            dma((blocks,)),
            dma((blocks,)),
            dma((blocks,)),
            dma((others,)),
            dma((others,)),
        ],
        compiler_params=pltpu.CompilerParams(
            collective_id=0, has_side_effects=True
        ),
        name="graph_layer",
    )(features, weight, cotangent, tile_values, tile_rows, tile_cols, tile_count)
    if not w_chunk:
        wgrad = lax.all_gather(lax.psum(wgrad, "blk"), "rep", axis=0, tiled=True)
    results = (act, wgrad, fgrad)
    return pl.pallas_call(
        publish,
        out_shape=tuple(jax.ShapeDtypeStruct(x.shape, x.dtype) for x in results),
        in_specs=[vmem] * 3,
        out_specs=(vmem,) * 3,
        name="publish",
    )(*results)


def solution(mesh):
    return jax.shard_map(
        per_device,
        mesh=mesh,
        in_specs=(
            P("blk", None),
            P(),
            P(("blk", "rep"), None),
            P("blk", "rep", None, None, None),
            P("blk", "rep", None),
            P("blk", "rep", None),
            P("blk", "rep"),
        ),
        out_specs=(P(("blk", "rep"), None), P(), P(("blk", "rep"), None)),
        check_vma=False,
    )
```

```python
import functools
import math

import jax
import jax.numpy as jnp
from jax import lax
from jax.experimental import pallas as pl
from jax.experimental.pallas import tpu as pltpu
from jax.sharding import PartitionSpec as P

MESH = pl.DeviceIdType.MESH
TILE = 128
UNROLL = 8
HALVES = 4


def repeat(count, body, first=0):
    if count - first <= UNROLL:
        for index in range(first, count):
            body(index)
    else:

        def step(index, carry):
            body(index)
            return carry

        lax.fori_loop(first, count, step, 0)


def kernel(dims, *refs):
    blocks, replicas, sections, rows_blk, width, slots, own_rows, w_rows, w_chunk, nodes = dims
    (feat, weight_hbm, cot_hbm, tiles_hbm, trows_hbm, tcols_hbm, tcount_hbm) = refs[:7]
    (act, wgrad, fgrad) = refs[7:10]
    (weight, cot, tiles, trows, tcols, tcount) = refs[10:16]
    (fbuf, amat, amat_t, pbuf, rbuf, dzfull, agg_t, aggs) = refs[16:24]
    (gsend, gpair, gbuf, gslots, wpart, wslots, wcol) = refs[24:31]
    (pfull, weight_t, gterm, wmine, wall, fown) = refs[31:37]
    (s_sem, l_sem) = refs[37:39]
    (f_send, f_recv, h_send, h_recv, p_send, p_recv, z_send, z_recv, a_send, a_recv) = refs[39:49]
    (o_send, o_recv, g_send, g_recv, w_send, w_recv, c_send, c_recv, r_send, r_recv) = refs[49:]
    b = lax.axis_index("blk")
    r = lax.axis_index("rep")
    odd = lax.rem(b, 2)
    pairs = sections // 2
    row_tiles = rows_blk // TILE
    column_parts = width // TILE
    whole_weight = w_chunk > 0
    pieces = [(c, h) for c in range(column_parts) for h in range(HALVES)]

    def blk_at(offset):
        return lax.rem(b + offset + 2 * blocks, blocks)

    def remote(src, dst, send, recv, to):
        return pltpu.make_async_remote_copy(
            src_ref=src, dst_ref=dst, send_sem=send, recv_sem=recv, device_id=to, device_id_type=MESH
        )

    local = [
        pltpu.make_async_copy(src, dst, l_sem.at[n])
        for n, (src, dst) in enumerate(
            (
                (trows_hbm, trows),
                (tcols_hbm, tcols),
                (tcount_hbm, tcount),
                (tiles_hbm, tiles),
                (weight_hbm, weight),
                (cot_hbm, cot),
            )
        )
    ]
    loads = [
        pltpu.make_async_copy(feat.at[:, pl.ds(c * TILE, TILE)], fown.at[c], s_sem.at[c])
        for c in range(column_parts)
    ]
    for copy in loads + local:
        copy.start()

    barrier = pltpu.get_barrier_semaphore()

    def greet(to):
        pl.semaphore_signal(barrier, inc=1, device_id=to, device_id_type=MESH)

    neighbour = b + 1 - 2 * odd
    repeat(replicas, lambda d: greet((b, lax.rem(r + d, replicas))), 1)
    repeat(blocks, lambda d: greet((blk_at(d), r)), 1)
    greet((neighbour, lax.rem(r + 2 * odd - 1 + replicas, replicas)))

    def greet_grad(j):
        @pl.when(jnp.logical_or(j != 0, r != 0))
        def _():
            greet((blk_at(-2 * j), 2 * j // sections))

    repeat(blocks // 2, greet_grad)
    own = jnp.where(r == 0, 1, 0)
    pl.semaphore_wait(barrier, replicas + blocks - 1 + pairs * replicas - own)

    half_rows = rows_blk // HALVES

    def piece(section, c, h):
        return fbuf.at[section, c, pl.ds(h * half_rows, half_rows)]

    def feature_piece(c, h):
        return fown.at[c, pl.ds(h * half_rows, half_rows)]

    def feature_copy(t, c, h):
        return remote(
            feature_piece(c, h),
            piece(2 * t, c, h),
            f_send.at[t, c, h],
            f_recv.at[t, c, h],
            (blk_at(-(sections * r + 2 * t)), r),
        )

    def feature_local(c, h):
        return pltpu.make_async_copy(feature_piece(c, h), piece(0, c, h), f_recv.at[0, c, h])

    def hand_copy(t, c, h):
        section = lax.rem(2 * t + 2 * odd - 1 + sections, sections)
        back = jnp.where(odd == 0, 1, 0) if t == 0 else 0
        return remote(
            piece(2 * t, c, h),
            piece(section, c, h),
            h_send.at[t, c, h],
            h_recv.at[section // 2, c, h],
            (neighbour, lax.rem(r - back + replicas, replicas)),
        )

    def hand_arrival(t, c, h):
        here = piece(2 * t + 1, c, h)
        return remote(here, here, h_send.at[t, c, h], h_recv.at[t, c, h], (neighbour, r))

    for c, h in pieces:
        if h == 0:
            loads[c].wait()
        for t in range(pairs):
            if t == 0:

                @pl.when(r != 0)
                def _():
                    feature_copy(0, c, h).start()

                @pl.when(r == 0)
                def _():
                    feature_local(c, h).start()
            else:
                feature_copy(t, c, h).start()

    for copy in local[:4]:
        copy.wait()

    def place_tiles(s):
        count = tcount[0, s]
        place = [
            jnp.where(t < count, trows[0, s, t] * row_tiles + tcols[0, s, t], -1)
            for t in range(slots)
        ]
        for i in range(row_tiles):
            for j in range(row_tiles):
                slot = jnp.int32(0)
                for t in range(slots):
                    slot = jnp.where(place[t] == i * row_tiles + j, t + 1, slot)
                tile = tiles[0, s, jnp.maximum(slot - 1, 0)]
                tile = jnp.where(slot > 0, tile, jnp.zeros_like(tile))
                at_col = pl.ds(s * rows_blk + j * TILE, TILE)
                amat[pl.ds(i * TILE, TILE), at_col] = tile

    def turn_tiles(s):
        for i in range(row_tiles):
            for j in range(row_tiles):
                at_row = pl.ds(i * TILE, TILE)
                at_col = pl.ds(s * rows_blk + j * TILE, TILE)
                amat_t[at_col, at_row] = amat[at_row, at_col].T

    for s in range(pairs):
        place_tiles(s)
    for n, (c, h) in enumerate(pieces):
        for t in range(pairs):
            if t == 0:

                @pl.when(r != 0)
                def _():
                    feature_copy(0, c, h).wait()

                @pl.when(r == 0)
                def _():
                    feature_local(c, h).wait()
            else:
                feature_copy(t, c, h).wait()
            hand_copy(t, c, h).start()
        if n == 0:
            for s in range(pairs, sections):
                place_tiles(s)
        if n == HALVES - 1:
            for s in range(1, sections, 2):
                turn_tiles(s)

    def rows_of(k):
        return pl.ds(pl.multiple_of(k * own_rows, own_rows), own_rows)

    def partial_copy(d, c):
        peer = lax.rem(r + d, replicas)
        return remote(
            pbuf.at[c, rows_of(peer)],
            rbuf.at[d - 1, c],
            p_send.at[d - 1, c],
            p_recv.at[d - 1, c],
            (b, peer),
        )

    totals = []
    for c in range(column_parts):
        for h in range(HALVES):
            for t in range(pairs):
                hand_arrival(t, c, h).wait_recv()
        product = jnp.zeros((rows_blk, TILE), jnp.float32)
        for s in range(sections):
            product = product + jnp.dot(
                amat[:, s * rows_blk : (s + 1) * rows_blk],
                fbuf[s, c],
                preferred_element_type=jnp.float32,
            )
        pbuf[c] = product.astype(pbuf.dtype)
        repeat(replicas, lambda d: partial_copy(d, c).start(), 1)
        pfull[...] = product
        totals.append(pfull[rows_of(r), :])
        if c == 0:
            for s in range(0, sections, 2):
                turn_tiles(s)
    for copy in local[4:]:
        copy.wait()
    weight_t[...] = weight[...].T
    for c in range(column_parts):
        repeat(replicas, lambda d: partial_copy(d, c).wait(), 1)
        for d in range(1, replicas):
            totals[c] = totals[c] + rbuf[d - 1, c].astype(jnp.float32)
    agg = jnp.concatenate(totals, axis=1).astype(jnp.bfloat16)

    z_value = jnp.dot(agg, weight[...], preferred_element_type=jnp.float32)
    sigma = jax.nn.sigmoid(z_value)
    dz = (cot[...].astype(jnp.float32) * sigma * (1.0 + z_value * (1.0 - sigma))).astype(jnp.bfloat16)
    mine = pl.ds(pl.multiple_of(r * own_rows, own_rows), own_rows)
    dzfull[mine, :] = dz

    def dz_copy(d):
        return remote(
            dzfull.at[mine],
            dzfull.at[mine],
            z_send.at[d - 1],
            z_recv.at[d - 1],
            (b, lax.rem(r + d, replicas)),
        )

    def dz_arrival(d):
        source = lax.rem(r + replicas - d, replicas)
        at_row = pl.ds(pl.multiple_of(source * own_rows, own_rows), own_rows)
        return remote(
            dzfull.at[at_row], dzfull.at[at_row], z_send.at[d - 1], z_recv.at[d - 1], (b, source)
        )

    repeat(replicas, lambda d: dz_copy(d).start(), 1)
    agg_t[...] = agg.T

    def agg_copy(d):
        peer = lax.rem(r + d, replicas)
        at_row = pl.ds(pl.multiple_of(peer * w_rows, w_rows), w_rows)
        return remote(agg_t.at[at_row], aggs.at[d], a_send.at[d - 1], a_recv.at[d - 1], (b, peer))

    repeat(replicas, lambda d: agg_copy(d).start(), 1)
    aggs[0] = agg_t[pl.ds(pl.multiple_of(r * w_rows, w_rows), w_rows), :]
    act[...] = (z_value * sigma).astype(jnp.bfloat16)

    repeat(replicas, lambda d: dz_arrival(d).wait_recv(), 1)
    dy = jnp.dot(dzfull[...], weight_t[...], preferred_element_type=jnp.float32).astype(jnp.bfloat16)

    def grad_terms(s):
        at_row = pl.ds(s * rows_blk, rows_blk)
        return jnp.dot(amat_t[at_row, :], dy, preferred_element_type=jnp.float32)

    def odd_copy(t, k):
        slot = lax.rem(t + odd, pairs)
        ahead = odd if t == pairs - 1 else 0
        return remote(
            gsend.at[t, k],
            gpair.at[slot, k],
            o_send.at[t, k],
            o_recv.at[slot, k],
            (neighbour, lax.rem(r + ahead, replicas)),
        )

    def odd_arrival(t, k):
        here = gpair.at[t, k]
        return remote(here, here, o_send.at[t, k], o_recv.at[t, k], (neighbour, r))

    def grad_copy(t, k):
        j = pairs * r + t
        return remote(
            gbuf.at[t, k], gslots.at[j], g_send.at[t, k], g_recv.at[j], (blk_at(2 * j), k)
        )

    def send_grad(t, k):
        term = gterm[t, k]
        odd_arrival(t, k).wait_recv()
        gbuf[t, k] = (term + gpair[t, k].astype(jnp.float32)).astype(gbuf.dtype)
        if t == 0 and k == 0:

            @pl.when(r != 0)
            def _():
                grad_copy(t, k).start()

            @pl.when(r == 0)
            def _():
                gslots[0] = gbuf[0, 0]
        else:
            grad_copy(t, k).start()

    def weight_rows():
        repeat(replicas, lambda d: agg_copy(d).wait_recv(), 1)
        acc = jnp.zeros((w_rows, width), jnp.float32)
        for d in range(replicas):
            source = lax.rem(r + replicas - d, replicas)
            at_row = pl.ds(pl.multiple_of(source * own_rows, own_rows), own_rows)
            acc = acc + jnp.dot(aggs[d], dzfull[at_row, :], preferred_element_type=jnp.float32)
        return acc * (1.0 / math.sqrt(nodes))

    def chunk_of(at):
        return pl.ds(pl.multiple_of(at * w_chunk, w_chunk), w_chunk)

    def w_copy(d):
        return remote(
            wpart.at[chunk_of(blk_at(d))], wslots.at[d - 1], w_send.at[d - 1], w_recv.at[d - 1], (blk_at(d), r)
        )

    def c_copy(d):
        return remote(
            wcol.at[chunk_of(b)], wcol.at[chunk_of(b)], c_send.at[d - 1], c_recv.at[d - 1], (blk_at(d), r)
        )

    def c_arrival(d):
        at_row = chunk_of(blk_at(-d))
        return remote(wcol.at[at_row], wcol.at[at_row], c_send.at[d - 1], c_recv.at[d - 1], (blk_at(-d), r))

    def r_copy(d):
        at_row = pl.ds(pl.multiple_of(r * w_rows, w_rows), w_rows)
        return remote(
            wmine, wall.at[at_row], r_send.at[d - 1], r_recv.at[d - 1], (b, lax.rem(r + d, replicas))
        )

    def r_arrival(d):
        source = lax.rem(r + replicas - d, replicas)
        at_row = pl.ds(pl.multiple_of(source * w_rows, w_rows), w_rows)
        return remote(wmine, wall.at[at_row], r_send.at[d - 1], r_recv.at[d - 1], (b, source))

    def weight_sum():
        repeat(blocks, lambda d: w_copy(d).wait_recv(), 1)
        chunk = wpart[chunk_of(b), :]
        for d in range(1, blocks):
            chunk = chunk + wslots[d - 1]
        wcol[chunk_of(b), :] = chunk
        repeat(blocks, lambda d: c_copy(d).start(), 1)

    def weight_gather():
        repeat(blocks, lambda d: c_arrival(d).wait_recv(), 1)
        wmine[...] = wcol[...].astype(wmine.dtype)
        repeat(replicas, lambda d: r_copy(d).start(), 1)

    odd_first = grad_terms(1).astype(gsend.dtype).reshape(gsend.shape[1:])
    gsend[0] = odd_first
    early = replicas // 2
    for k in range(early):
        odd_copy(0, k).start()
    if whole_weight:
        wpart[...] = weight_rows()
        repeat(blocks, lambda d: w_copy(d).start(), 1)
    else:
        wgrad[...] = weight_rows()
    for k in range(early, replicas):
        odd_copy(0, k).start()
    for t in range(1, pairs):
        gsend[t] = grad_terms(2 * t + 1).astype(gsend.dtype).reshape(gsend.shape[1:])
        for k in range(replicas):
            odd_copy(t, k).start()
    for t in range(pairs):
        gterm[t] = grad_terms(2 * t).reshape(gterm.shape[1:])

    for t in range(pairs):
        for k in range(replicas):
            send_grad(t, k)
            if whole_weight and t == pairs - 1 and k == early - 1:
                weight_sum()
    if whole_weight:
        weight_gather()

    def grad_arrival(j):
        copy = remote(
            gslots.at[j], gslots.at[j], g_send.at[0, 0], g_recv.at[j], (blk_at(-2 * j), j // pairs)
        )

        @pl.when(jnp.logical_or(j != 0, r != 0))
        def _():
            copy.wait_recv()

    repeat(blocks // 2, grad_arrival)
    summed = gslots[0].astype(jnp.float32)
    for j in range(1, blocks // 2):
        summed = summed + gslots[j].astype(jnp.float32)
    fgrad[...] = summed.astype(jnp.bfloat16)

    if whole_weight:
        at_row = pl.ds(pl.multiple_of(r * w_rows, w_rows), w_rows)
        wall[at_row, :] = wmine[...]
        repeat(replicas, lambda d: r_arrival(d).wait_recv(), 1)
        wgrad[...] = wall[...].astype(jnp.float32)

    for t in range(pairs):
        for c, h in pieces:
            hand_copy(t, c, h).wait_send()
    repeat(replicas, lambda d: dz_copy(d).wait_send(), 1)
    repeat(replicas, lambda d: agg_copy(d).wait_send(), 1)
    for t in range(pairs):
        for k in range(replicas):
            odd_copy(t, k).wait_send()
            if t == 0 and k == 0:

                @pl.when(r != 0)
                def _():
                    grad_copy(t, k).wait_send()
            else:
                grad_copy(t, k).wait_send()
    if whole_weight:
        repeat(blocks, lambda d: w_copy(d).wait_send(), 1)
        repeat(blocks, lambda d: c_copy(d).wait_send(), 1)
        repeat(replicas, lambda d: r_copy(d).wait_send(), 1)


def publish(*refs):
    for n in range(3):
        refs[3 + n][...] = refs[n][...]


def per_device(features, weight, cotangent, tile_values, tile_rows, tile_cols, tile_count):
    rows_blk, width = features.shape
    sections, slots = tile_rows.shape[1:]
    replicas = lax.axis_size("rep")
    blocks = lax.axis_size("blk")
    nodes = rows_blk * blocks
    own_rows = rows_blk // replicas
    w_rows = width // replicas
    w_chunk = w_rows // blocks if w_rows % (8 * blocks) == 0 else 0
    dims = (blocks, replicas, sections, rows_blk, width, slots, own_rows, w_rows, w_chunk, nodes)
    bf16, f32 = jnp.bfloat16, jnp.float32
    vmem = pl.BlockSpec(memory_space=pltpu.VMEM)
    dma = pltpu.SemaphoreType.DMA
    others = max(replicas - 1, 1)
    pairs, parts = sections // 2, width // TILE
    act, wgrad, fgrad = pl.pallas_call(
        functools.partial(kernel, dims),
        out_shape=(
            jax.ShapeDtypeStruct((own_rows, width), bf16),
            jax.ShapeDtypeStruct((width if w_chunk else w_rows, width), f32),
            jax.ShapeDtypeStruct((own_rows, width), bf16),
        ),
        in_specs=[pl.BlockSpec(memory_space=pltpu.HBM)] * 7,
        out_specs=(vmem, vmem, vmem),
        scratch_shapes=[
            pltpu.VMEM(weight.shape, bf16),
            pltpu.VMEM(cotangent.shape, bf16),
            pltpu.VMEM(tile_values.shape, bf16),
            pltpu.SMEM(tile_rows.shape, jnp.int32),
            pltpu.SMEM(tile_cols.shape, jnp.int32),
            pltpu.SMEM(tile_count.shape, jnp.int32),
            pltpu.VMEM((sections, parts, rows_blk, TILE), bf16),
            pltpu.VMEM((rows_blk, sections * rows_blk), bf16),
            pltpu.VMEM((sections * rows_blk, rows_blk), bf16),
            pltpu.VMEM((parts, rows_blk, TILE), bf16),
            pltpu.VMEM((others, parts, own_rows, TILE), bf16),
            pltpu.VMEM((rows_blk, width), bf16),
            pltpu.VMEM((width, own_rows), bf16),
            pltpu.VMEM((replicas, w_rows, own_rows), bf16),
            pltpu.VMEM((pairs, replicas, own_rows, width), bf16),
            pltpu.VMEM((pairs, replicas, own_rows, width), bf16),
            pltpu.VMEM((pairs, replicas, own_rows, width), bf16),
            pltpu.VMEM((blocks // 2, own_rows, width), bf16),
            pltpu.VMEM((w_rows, width), f32),
            pltpu.VMEM((blocks, max(w_chunk, 8), width), f32),
            pltpu.VMEM((w_rows, width), f32),
            pltpu.VMEM((rows_blk, TILE), f32),
            pltpu.VMEM(weight.shape, bf16),
            pltpu.VMEM((pairs, replicas, own_rows, width), f32),
            pltpu.VMEM((w_rows, width), bf16),
            pltpu.VMEM((width, width), bf16),
            pltpu.VMEM((parts, rows_blk, TILE), bf16),
            dma((parts,)),
            dma((6,)),
            dma((pairs, parts, HALVES)),
            dma((pairs, parts, HALVES)),
            dma((pairs, parts, HALVES)),
            dma((pairs, parts, HALVES)),
            dma((others, parts)),
            dma((others, parts)),
            dma((others,)),
            dma((others,)),
            dma((others,)),
            dma((others,)),
            dma((pairs, replicas)),
            dma((pairs, replicas)),
            dma((pairs, replicas)),
            dma((blocks // 2,)),
            dma((blocks,)),
            dma((blocks,)),
            dma((blocks,)),
            dma((blocks,)),
            dma((others,)),
            dma((others,)),
        ],
        compiler_params=pltpu.CompilerParams(
            collective_id=0, has_side_effects=True
        ),
        name="graph_layer",
    )(features, weight, cotangent, tile_values, tile_rows, tile_cols, tile_count)
    if not w_chunk:
        wgrad = lax.all_gather(lax.psum(wgrad, "blk"), "rep", axis=0, tiled=True)
    results = (act, wgrad, fgrad)
    return pl.pallas_call(
        publish,
        out_shape=tuple(jax.ShapeDtypeStruct(x.shape, x.dtype) for x in results),
        in_specs=[vmem] * 3,
        out_specs=(vmem,) * 3,
        name="publish",
    )(*results)


def solution(mesh):
    return jax.shard_map(
        per_device,
        mesh=mesh,
        in_specs=(
            P("blk", None),
            P(),
            P(("blk", "rep"), None),
            P("blk", "rep", None, None, None),
            P("blk", "rep", None),
            P("blk", "rep", None),
            P("blk", "rep"),
        ),
        out_specs=(P(("blk", "rep"), None), P(), P(("blk", "rep"), None)),
        check_vma=False,
    )
```
